32 devices in a mesh: dp: 8 (over y, x, core), head: 4 (over z).
Axes of the slice: x: 2, y: 2, z: 4, core: 2. Of those that a mesh axis runs over, the one named last changes fastest.
Arguments:
- block_input: bfloat16 [2, 4096, 2048], P(None, 'dp', 'head'), may hold values from -6 to 6
- cotangent: bfloat16 [2, 4096, 2048], P(None, 'dp'), may hold values from -6 to 6
- seq_count: int32 [2, 8], P(None, 'dp'), may hold values from 1 to 2, as said below
- attn_gain: bfloat16 [2048], P('head'), may hold values from 0.5 to 1.5
- w_query: bfloat16 [2048, 2048], P(None, 'head'), may hold values from -0.125 to 0.125
- w_key: bfloat16 [2048, 2048], P(None, 'head'), may hold values from -0.125 to 0.125
- w_value: bfloat16 [2048, 2048], P(None, 'head'), may hold values from -0.125 to 0.125
- w_gate: bfloat16 [2048, 2048], P(None, 'head'), may hold values from -0.125 to 0.125
- w_alpha: bfloat16 [2048, 16], P(None, 'head'), may hold values from -0.125 to 0.125
- w_beta: bfloat16 [2048, 16], P(None, 'head'), may hold values from -0.125 to 0.125
- conv_weight: float32 [3, 4, 2048], P(None, None, 'head'), may hold values from -3 to 3
- decay_base: float32 [16], P('head'), may hold values from 0 to 2.5
- decay_bias: float32 [16], P('head'), may hold values from -5 to -2
- norm_gain: float32 [128], replicated, may hold values from 0.5 to 1.5
- w_out: bfloat16 [2048, 2048], P('head'), may hold values from -0.125 to 0.125
- mlp_gain: bfloat16 [2048], P('head'), may hold values from 0.5 to 1.5
- w_mlp_gate: bfloat16 [2048, 5632], P(None, 'head'), may hold values from -0.125 to 0.125
- w_mlp_up: bfloat16 [2048, 5632], P(None, 'head'), may hold values from -0.125 to 0.125
- w_down: bfloat16 [5632, 2048], P('head'), may hold values from -0.078125 to 0.078125
Outputs:
- output: bfloat16 [2, 4096, 2048], P(None, 'dp', 'head')
- grad_input: float32 [2, 4096, 2048], P(None, 'dp', 'head')
- grad_attn_gain: float32 [2048], P('head')
- grad_w_query: float32 [2048, 2048], P('dp', 'head')
- grad_w_key: float32 [2048, 2048], P('dp', 'head')
- grad_w_value: float32 [2048, 2048], P('dp', 'head')
- grad_w_gate: float32 [2048, 2048], P('dp', 'head')
- grad_w_alpha: float32 [2048, 16], P('dp', 'head')
- grad_w_beta: float32 [2048, 16], P('dp', 'head')
- grad_conv_weight: float32 [3, 4, 2048], P(None, None, 'head')
- grad_decay_base: float32 [16], P('head')
- grad_decay_bias: float32 [16], P('head')
- grad_norm_gain: float32 [128], replicated
- grad_w_out: float32 [2048, 2048], P('head', 'dp')
- grad_mlp_gain: float32 [2048], P('head')
- grad_w_mlp_gate: float32 [2048, 5632], P('dp', 'head')
- grad_w_mlp_up: float32 [2048, 5632], P('dp', 'head')
- grad_w_down: float32 [5632, 2048], P('head', 'dp')
The draws below stay inside these ranges and needn't reach their ends.
Inputs may be any that keep to these rules, and one draw needn't show every extreme that they name: seq_count[m, g] counts the sequences that fill the first slots of data group g in micro-batch m; the rows of the other slots are ignored. In every micro-batch some group has 2.
All inputs are finite; a program needn't handle non-finite values.
Results may differ from the reference program's by a relative error of at most 0.014.
Values may be sent and summed in bfloat16 or wider, within the bound.
No kernel may reach another device: no remote copies, remote signals or barrier semaphores. Data moves between devices by JAX's collectives and lax.ppermute only.
A program may use at most 320 MiB of HBM per device.

```python
import jax
import jax.numpy as jnp
from jax import lax

D = 2048
H = 16
DK = 128
FF = 5632
CONV = 4
SPAN = 64
SEQ = 256
SLOTS = 2
MB = 2
HD = 2048
ROWS = 512
TOKENS = 4096
N_DP = 8


def draw_seq_count(key, part):
    first_key = jax.random.fold_in(key, 11)
    second_key = jax.random.fold_in(key, 23)
    counts = jax.random.randint(first_key, (MB, N_DP), 1, SLOTS + 1)
    busiest = jax.random.randint(second_key, (MB, 1), 0, N_DP)
    return jnp.where(jnp.arange(N_DP)[None, :] == busiest, SLOTS, counts).astype(jnp.int32)


def steps_of(stream_key, dims, split, least, high):
    loudness, own = 1.0, jax.random.fold_in(stream_key, 6)
    for axis_at, parts in split:
        draws = jnp.exp(jax.random.uniform(jax.random.fold_in(own, axis_at), (parts,), jnp.float32, least / len(split), high / len(split)))
        loudness = loudness * jnp.repeat(draws, dims[axis_at] // parts).reshape([-1 if axis == axis_at else 1 for axis in range(len(dims))])
    return loudness


def normal_values(key, dims, width, limit, cuts=(), dtype=jnp.bfloat16):
    entries = jax.random.normal(key, dims, jnp.float32) * width
    if len(cuts) > 0:
        entries = steps_of(key, dims, cuts, -0.22, 0.18) * entries
    return jnp.clip(entries, min=-limit, max=limit).astype(dtype)


def setup_inputs(seed: int = 0) -> dict:
    key_of = jax.random.split(jax.random.key(seed), 20)
    return {
        "block_input": normal_values(key_of[0], (MB, TOKENS, D), 1.0, 6.0, ((1, 8), (2, 4))),
        "cotangent": normal_values(key_of[1], (MB, TOKENS, D), 1.0, 6.0, ((1, 8),)),
        "seq_count": draw_seq_count(jax.random.fold_in(key_of[19], 71), 0),
        "attn_gain": jnp.clip(1.0 + 0.1 * jax.random.normal(key_of[3], (D,), jnp.float32), 0.5, 1.5).astype(jnp.bfloat16),
        "w_query": normal_values(key_of[4], (D, HD), D ** -0.5, 0.125, ((1, 4),)),
        "w_key": normal_values(key_of[5], (D, HD), D ** -0.5, 0.125, ((1, 4),)),
        "w_value": normal_values(key_of[6], (D, HD), D ** -0.5, 0.125, ((1, 4),)),
        "w_gate": normal_values(key_of[7], (D, HD), D ** -0.5, 0.125, ((1, 4),)),
        "w_alpha": normal_values(key_of[8], (D, H), D ** -0.5, 0.125, ((1, 4),)),
        "w_beta": normal_values(key_of[9], (D, H), D ** -0.5, 0.125, ((1, 4),)),
        "conv_weight": normal_values(key_of[10], (3, CONV, HD), CONV ** -0.5, 3.0, ((2, 4),), jnp.float32),
        "decay_base": jnp.clip(2.5 * jax.random.uniform(key_of[11], (H,), jnp.float32) ** steps_of(key_of[11], (H,), ((0, 4),), -0.2, 0.2), 0.0, 2.5),
        "decay_bias": jnp.clip(-5.0 + 3.0 * jax.random.uniform(key_of[12], (H,), jnp.float32) ** steps_of(key_of[12], (H,), ((0, 4),), -0.2, 0.2), -5.0, -2.0),
        "norm_gain": jnp.clip(1.0 + 0.1 * jax.random.normal(key_of[13], (DK,), jnp.float32), 0.5, 1.5),
        "w_out": normal_values(key_of[14], (HD, D), HD ** -0.5, 0.125, ((0, 4),)),
        "mlp_gain": jnp.clip(1.0 + 0.1 * jax.random.normal(key_of[15], (D,), jnp.float32), 0.5, 1.5).astype(jnp.bfloat16),
        "w_mlp_gate": normal_values(key_of[16], (D, FF), D ** -0.5, 0.125, ((1, 4),)),
        "w_mlp_up": normal_values(key_of[17], (D, FF), D ** -0.5, 0.125, ((1, 4),)),
        "w_down": normal_values(key_of[18], (FF, D), FF ** -0.5, 0.078125, ((0, 4),)),
    }


epsilon = 1e-06
highest_precision = lax.Precision.HIGHEST

@jax.custom_vjp
def low(v):
    return lax.optimization_barrier(v.astype(jnp.bfloat16)).astype(jnp.float32)

@jax.custom_vjp
def low_back(v):
    return v

def low_keep(v):
    return (low(v), None)

def low_pass(kept, grad):
    return (grad,)

def back_keep(v):
    return (v, None)

def back_low(kept, grad):
    return (low(grad),)
low.defvjp(low_keep, low_pass)
low_back.defvjp(back_keep, back_low)

def matmul(former, latter):
    return jnp.dot(former, latter, precision=highest_precision, preferred_element_type=jnp.float32)

def short_conv(values, weights):
    padded = jnp.pad(values, ((0, 0), (CONV - 1, 0), (0, 0)))
    summed = jnp.zeros_like(values)
    for offset in range(CONV):
        summed = summed + padded[:, offset:offset + SEQ] * weights[offset]
    return jax.nn.silu(summed)

def unit_rows(values, factor):
    return values * lax.rsqrt(lax.optimization_barrier(jnp.sum(values * values, -1, keepdims=True)) + epsilon) * factor

def delta_step(memory_state, inputs_now):
    queries, key_rows, value_rows, decay_log, strength = inputs_now
    projected = jnp.einsum('bhk,bhkv->bhv', key_rows, memory_state, precision=highest_precision)
    keep_now = jnp.exp(decay_log)[:, :, None, None]
    write_now = strength[:, :, None, None]
    memory_state = keep_now * (memory_state - write_now * key_rows[:, :, :, None] * projected[:, :, None, :]) + write_now * key_rows[:, :, :, None] * value_rows[:, :, None, :]
    return (memory_state, jnp.einsum('bhk,bhkv->bhv', queries, memory_state, precision=highest_precision))

def delta_block(memory_state, block_inputs):
    return lax.scan(delta_step, memory_state, block_inputs)

def recurrence(queries, key_rows, value_rows, decay_log, strength):

    def to_blocks(values):
        moved = jnp.swapaxes(values, 0, 1)
        return moved.reshape((SEQ // SPAN, SPAN) + moved.shape[1:])
    memory_state = jnp.zeros((SLOTS, H, DK, DK), jnp.float32)
    inputs_all = (to_blocks(queries), to_blocks(key_rows), to_blocks(value_rows), to_blocks(decay_log), to_blocks(strength))
    memory_state, outputs = lax.scan(jax.checkpoint(delta_block), memory_state, inputs_all)
    return jnp.swapaxes(outputs.reshape((SEQ, SLOTS, H, DK)), 0, 1)

def mixer(query_pre, key_pre, value_pre, gate_pre, alpha_pre, beta_pre, conv_weight, decay_base, decay_bias, norm_gain):

    def slotted(values):
        return values.reshape((SLOTS, SEQ) + values.shape[1:])
    shaped = (SLOTS, SEQ, H, DK)
    queries = unit_rows(short_conv(slotted(query_pre), conv_weight[0]).reshape(shaped), DK ** (-0.5))
    key_rows = unit_rows(short_conv(slotted(key_pre), conv_weight[1]).reshape(shaped), 1.0)
    value_rows = short_conv(slotted(value_pre), conv_weight[2]).reshape(shaped)
    decay_log = -jnp.exp(decay_base) * jax.nn.softplus(slotted(alpha_pre) + decay_bias)
    strength = jax.nn.sigmoid(slotted(beta_pre))
    delta_out = recurrence(queries, key_rows, value_rows, decay_log, strength)
    normed = delta_out * lax.rsqrt(lax.optimization_barrier(jnp.mean(delta_out * delta_out, -1, keepdims=True)) + epsilon) * norm_gain
    return (normed * jax.nn.silu(slotted(gate_pre).reshape(shaped))).reshape(ROWS, HD)

def layer(params, inputs):
    attn_gain, w_query, w_key, w_value, w_gate, w_alpha, w_beta, conv_weight, decay_base, decay_bias, norm_gain, w_out, mlp_gain, w_mlp_gate, w_mlp_up, w_down = params
    scale_in = lax.rsqrt(lax.optimization_barrier(jnp.mean(inputs * inputs, -1, keepdims=True)) + epsilon)
    normed = low(inputs * scale_in * attn_gain)
    query_pre = low_back(matmul(normed, w_query))
    key_pre = low_back(matmul(normed, w_key))
    value_pre = low_back(matmul(normed, w_value))
    gate_pre = low_back(matmul(normed, w_gate))
    alpha_pre = low_back(matmul(normed, w_alpha))
    beta_pre = low_back(matmul(normed, w_beta))
    mixed = low(mixer(query_pre, key_pre, value_pre, gate_pre, alpha_pre, beta_pre, conv_weight, decay_base, decay_bias, norm_gain))
    attended = low_back(matmul(mixed, w_out))
    hidden = inputs + attended
    scale_mid = lax.rsqrt(lax.optimization_barrier(jnp.mean(hidden * hidden, -1, keepdims=True)) + epsilon)
    normed_mid = low(hidden * scale_mid * mlp_gain)
    gate_act = low_back(matmul(normed_mid, w_mlp_gate))
    up_act = low_back(matmul(normed_mid, w_mlp_up))
    product = low(jax.nn.silu(gate_act) * up_act)
    return hidden + low_back(matmul(product, w_down))

def reference(block_input, cotangent, seq_count, attn_gain, w_query, w_key, w_value, w_gate, w_alpha, w_beta, conv_weight, decay_base, decay_bias, norm_gain, w_out, mlp_gain, w_mlp_gate, w_mlp_up, w_down):
    params = tuple((member.astype(jnp.float32) for member in (attn_gain, w_query, w_key, w_value, w_gate, w_alpha, w_beta, conv_weight, decay_base, decay_bias, norm_gain, w_out, mlp_gain, w_mlp_gate, w_mlp_up, w_down)))
    blocks_in = block_input.reshape(MB * N_DP, ROWS, D)
    blocks_back = cotangent.reshape(MB * N_DP, ROWS, D)
    counts = seq_count.reshape(MB * N_DP).astype(jnp.int32)

    def one_block(totals, slices):
        inputs, grad_out, live_count = slices
        live_rows = (jnp.arange(ROWS).astype(jnp.int32) // SEQ < live_count)[:, None]
        inputs = jnp.where(live_rows, inputs.astype(jnp.float32), 0.0)
        outputs, pullback = jax.vjp(layer, params, inputs)
        grad_params, grad_inputs = pullback(jnp.where(live_rows, grad_out.astype(jnp.float32), 0.0))
        totals = jax.tree.map(lambda former, latter: former + latter, totals, grad_params)
        return (totals, (outputs.astype(jnp.bfloat16), grad_inputs))
    totals, (outputs, grad_inputs) = lax.scan(one_block, jax.tree.map(jnp.zeros_like, params), (blocks_in, blocks_back, counts))
    grad_attn_gain, grad_w_query, grad_w_key, grad_w_value, grad_w_gate, grad_w_alpha, grad_w_beta, grad_conv_weight, grad_decay_base, grad_decay_bias, grad_norm_gain, grad_w_out, grad_mlp_gain, grad_w_mlp_gate, grad_w_mlp_up, grad_w_down = totals
    return (outputs.reshape(MB, TOKENS, D), grad_inputs.reshape(MB, TOKENS, D), grad_attn_gain, grad_w_query, grad_w_key, grad_w_value, grad_w_gate, grad_w_alpha, grad_w_beta, grad_conv_weight, grad_decay_base, grad_decay_bias, grad_norm_gain, grad_w_out, grad_mlp_gain, grad_w_mlp_gate, grad_w_mlp_up, grad_w_down)
```

```python
import functools
import jax
import jax.numpy as jnp
from jax import lax
from jax.experimental import pallas as pl
from jax.experimental.pallas import tpu as pltpu
from jax.sharding import PartitionSpec as P

SEQ = 256
CH = 128
TAPS = 4
epsilon = 1e-06
f32 = jnp.float32
bf16 = jnp.bfloat16


def halves(x):
    high = x.astype(bf16)
    return high, (x - high.astype(f32)).astype(bf16)


def left(x):
    return jnp.concatenate(halves(x), axis=1)


def right(x):
    row = jnp.concatenate(halves(x), axis=1)
    return jnp.concatenate([row, row], axis=0)


def right_t(x):
    high, low = halves(x)
    return jnp.concatenate(
        [jnp.concatenate([high, high], axis=1), jnp.concatenate([low, low], axis=1)], axis=0
    )


def fold(r):
    return r[:, :CH] + r[:, CH:]


def mm(l, r):
    return fold(jnp.dot(l, r, preferred_element_type=f32))


def mm_t(l, r):
    return fold(lax.dot_general(l, r, (((1,), (1,)), ((), ())), preferred_element_type=f32))


def grids():
    row = lax.broadcasted_iota(jnp.int32, (CH, CH), 0)
    col = lax.broadcasted_iota(jnp.int32, (CH, CH), 1)
    return row, col


def sum_matrix(row, col):
    lower = (row >= col).astype(bf16)
    zero = jnp.zeros((CH, CH), bf16)
    return jnp.concatenate(
        [
            jnp.concatenate([lower, jnp.full((CH, CH), -1, bf16)], axis=1),
            jnp.concatenate([lower, zero], axis=1),
            jnp.concatenate([(row < col).astype(bf16), zero], axis=1),
        ],
        axis=0,
    )


def decay_sums(decay, row, col, sums):
    wide = jnp.broadcast_to(decay, (CH, CH))
    cut = jnp.where(row <= col, wide, 0.0)
    r = jnp.concatenate(
        [jnp.concatenate(halves(wide), axis=1), jnp.concatenate(halves(cut), axis=1)], axis=0
    )
    out = fold(jnp.dot(sums, r, preferred_element_type=f32))
    return out[:CH], out[CH : 2 * CH], out[2 * CH :]


def shifted(x, by, row):
    if by == 0:
        return x
    return jnp.where(row >= by, pltpu.roll(x, by, 0), 0.0)


def shifted_back(x, by, row):
    if by == 0:
        return x
    return jnp.where(row < SEQ - by, pltpu.roll(x, SEQ - by, 0), 0.0)


def sigmoid(x):
    return 1.0 / (1.0 + jnp.exp(-x))


def conv_sum(x, taps, row):
    total = x * taps[TAPS - 1 : TAPS]
    for by in range(1, TAPS):
        total = total + shifted(x, by, row) * taps[TAPS - 1 - by : TAPS - by]
    return total


def conv_back(x, grad, taps, row):
    grad_x = grad * taps[TAPS - 1 : TAPS]
    sums = [jnp.sum(grad * x, 0, keepdims=True)]
    for by in range(1, TAPS):
        grad_x = grad_x + shifted_back(grad, by, row) * taps[TAPS - 1 - by : TAPS - by]
        sums.append(jnp.sum(grad * shifted(x, by, row), 0, keepdims=True))
    return grad_x, jnp.concatenate(sums[::-1], axis=0)


def norm_of(x):
    return lax.rsqrt(jnp.sum(x * x, -1, keepdims=True) + epsilon)


def softplus(x):
    return jnp.maximum(x, 0.0) + jnp.log(1.0 + jnp.exp(-jnp.abs(x)))


def forward_kernel(
    pre_ref, conv_ref, decay_ref, gain_ref,
    mixed_ref, inverse_ref, update_ref, delta_ref,
):
    heads = decay_ref.shape[1]
    inner = heads * CH

    def piece(index, h):
        return slice(index * inner + h * CH, index * inner + (h + 1) * CH)

    row, col = grids()
    long_row = lax.broadcasted_iota(jnp.int32, (SEQ, CH), 0)
    sums = sum_matrix(row, col)
    within = row >= col
    eye = (row == col).astype(f32)
    ab = pre_ref[:, 4 * inner :]
    decay_all = -jnp.exp(decay_ref[0:1, :]) * softplus(ab[:, :heads] + decay_ref[1:2, :])
    strength_all = sigmoid(ab[:, heads : 2 * heads])
    systems, inverses, kept = [], [], []
    for h in range(heads):
        at = slice(h * CH, (h + 1) * CH)
        parts = []
        for index in range(3):
            pre = conv_sum(pre_ref[:, piece(index, h)], conv_ref[index][:, at], long_row)
            parts.append(pre * sigmoid(pre))
        queries = parts[0] * norm_of(parts[0]) * CH ** (-0.5)
        keys = parts[1] * norm_of(parts[1])
        for c in range(2):
            span = slice(c * CH, (c + 1) * CH)
            q, k, v = queries[span], keys[span], parts[2][span]
            spread, start, tail = decay_sums(decay_all[span, h : h + 1], row, col, sums)
            falloff = jnp.where(within, jnp.exp(jnp.minimum(spread, 0.0)), 0.0)
            k_left = left(k)
            both = mm_t(jnp.concatenate([k_left, left(q)], axis=0), right_t(k))
            beta = jnp.broadcast_to(strength_all[span, h : h + 1], (CH, CH))
            system = jnp.where(row > col, beta * falloff * both[:CH], 0.0)
            systems.append(system)
            inverses.append(
                eye - jnp.where((row // 2 == col // 2) & (row % 2 > col % 2), system, 0.0)
            )
            kept.append((q, k_left, v, k, beta, falloff * both[CH:], jnp.exp(start), jnp.exp(tail)))
    size = 2
    while size < CH:
        mask = (row // (2 * size) == col // (2 * size)) & ((row // size) % 2 > (col // size) % 2)
        for i in range(len(systems)):
            inverse = inverses[i]
            step = mm(left(inverse), right(jnp.where(mask, systems[i], 0.0)))
            inverses[i] = inverse - mm(left(step), right(inverse))
        size *= 2
    for h in range(heads):
        at = slice(h * CH, (h + 1) * CH)
        q, k_left, v, k, beta, scores, start, tail = kept[2 * h]
        first_update = mm(left(inverses[2 * h]), right(beta * v))
        first_out = mm(left(scores), right(first_update))
        state = mm(left(k.T), right(tail * first_update))
        q, k_left, v, k, beta, scores, start, tail = kept[2 * h + 1]
        read = mm(jnp.concatenate([k_left, left(q)], axis=0), right(state))
        second_update = mm(left(inverses[2 * h + 1]), right(beta * (v - start * read[:CH])))
        second_out = start * read[CH:] + mm(left(scores), right(second_update))
        for c, (update, out) in enumerate(((first_update, first_out), (second_update, second_out))):
            span = slice(c * CH, (c + 1) * CH)
            update_ref[span, at] = update
            delta_ref[span, at] = out
            inverse_ref[span, at] = inverses[2 * h + c].T
            scale = lax.rsqrt(jnp.mean(out * out, -1, keepdims=True) + epsilon)
            gate = pre_ref[span, piece(3, h)]
            mixed_ref[span, at] = (
                out * scale * gain_ref[...] * (gate * sigmoid(gate))
            ).astype(bf16)


def backward_kernel(
    pre_ref, conv_ref, decay_ref, gain_ref,
    inverse_ref, update_ref, delta_ref, grad_ref,
    gpre_ref, gwide_ref, gdecay_ref,
):
    heads = decay_ref.shape[1]
    inner = heads * CH

    def piece(index, h):
        return slice(index * inner + h * CH, index * inner + (h + 1) * CH)

    row, col = grids()
    long_row = lax.broadcasted_iota(jnp.int32, (SEQ, CH), 0)
    sums = sum_matrix(row, col)
    within = row >= col
    strict = row > col
    upper = (row <= col).astype(bf16)
    upper2 = jnp.concatenate([upper, upper], axis=1)
    lower = strict.astype(bf16)
    lower2 = jnp.concatenate([lower, lower], axis=1)
    ab = pre_ref[:, 4 * inner :]
    rate = -jnp.exp(decay_ref[0:1, :])
    shift = ab[:, :heads] + decay_ref[1:2, :]
    decay_all = rate * softplus(shift)
    strength_all = sigmoid(ab[:, heads : 2 * heads])
    grad_decays, grad_strengths = [], []
    for h in range(heads):
        at = slice(h * CH, (h + 1) * CH)
        pres, parts = [], []
        for index in range(3):
            pre = conv_sum(pre_ref[:, piece(index, h)], conv_ref[index][:, at], long_row)
            pres.append(pre)
            parts.append(pre * sigmoid(pre))
        q_norm, k_norm = norm_of(parts[0]), norm_of(parts[1])
        queries = parts[0] * q_norm * CH ** (-0.5)
        keys = parts[1] * k_norm
        out = delta_ref[:, at]
        gate = pre_ref[:, piece(3, h)]
        grad = grad_ref[:, at]
        gain = gain_ref[...]
        scale = lax.rsqrt(jnp.mean(out * out, -1, keepdims=True) + epsilon)
        sig = sigmoid(gate)
        scaled = out * scale
        gpre_ref[:, piece(3, h)] = (grad * scaled * gain * sig * (1.0 + gate * (1.0 - sig))).astype(bf16)
        grad_normed = grad * gate * sig
        norm_gain_sum = jnp.sum(grad_normed * scaled, 0, keepdims=True)
        grad_scaled = grad_normed * gain
        grad_out = scale * (
            grad_scaled - scaled * jnp.mean(grad_scaled * scaled, -1, keepdims=True)
        )
        stuff = []
        for c in range(2):
            span = slice(c * CH, (c + 1) * CH)
            q, k, v = queries[span], keys[span], parts[2][span]
            spread, start, tail = decay_sums(decay_all[span, h : h + 1], row, col, sums)
            falloff = jnp.where(within, jnp.exp(jnp.minimum(spread, 0.0)), 0.0)
            q_left, k_left = left(q), left(k)
            both = mm_t(jnp.concatenate([k_left, q_left], axis=0), right_t(k))
            beta = jnp.broadcast_to(strength_all[span, h : h + 1], (CH, CH))
            stuff.append(
                (q, k, v, falloff, both[:CH] * falloff, both[CH:] * falloff, beta,
                 jnp.exp(start), jnp.exp(tail), q_left, k_left)
            )
        carry = None
        grads_q, grads_k, grads_v, grads_g, grads_b = [None] * 2, [None] * 2, [None] * 2, [None] * 2, [None] * 2
        first_update = update_ref[0:CH, at]
        tail_update = stuff[0][8] * first_update
        state = mm(left(stuff[0][1].T), right(tail_update))
        for c in (1, 0):
            span = slice(c * CH, (c + 1) * CH)
            q, k, v, falloff, similar, scores, beta, start, tail, q_left, k_left = stuff[c]
            update = update_ref[span, at]
            go = grad_out[span]
            grad_update = mm(left(scores.T), right(go))
            target = v
            if c == 1:
                read = mm(jnp.concatenate([k_left, q_left], axis=0), right(state))
                target = v - start * read[:CH]
            else:
                pushed = mm(k_left, right(carry))
                grad_update = grad_update + tail * pushed
            grad_write = mm(left(inverse_ref[span, at]), right(grad_update))
            outer = mm_t(
                jnp.concatenate([left(grad_write), left(go)], axis=0), right_t(update)
            )
            grad_system = jnp.where(strict, -outer[:CH], 0.0)
            grad_scores = jnp.where(within, outer[CH:], 0.0)
            grads_b[c] = jnp.sum(grad_write * target + grad_system * similar, -1, keepdims=True)
            grad_target = beta * grad_write
            grads_v[c] = grad_target
            grad_similar = grad_system * beta * falloff
            grad_dots = grad_scores * falloff
            moved = grad_system * beta * similar + grad_scores * scores
            k_right = right(k)
            back = mm(
                jnp.concatenate(
                    [left(grad_dots), left(grad_similar + grad_similar.T)], axis=0
                ),
                k_right,
            )
            gq = back[:CH]
            gk = back[CH:] + mm(left(grad_dots.T), right(q))
            if c == 1:
                through_out, through_read = start * go, -start * grad_target
                more = mm_t(
                    jnp.concatenate([left(through_out), left(through_read)], axis=0),
                    right_t(state),
                )
                gq = gq + more[:CH]
                gk = gk + more[CH:]
                carry = mm(left(q.T), right(through_out)) + mm(left(k.T), right(through_read))
                other = through_out * read[CH:] + through_read * read[:CH]
                turned = jnp.dot(
                    upper2,
                    jnp.concatenate(
                        [
                            jnp.concatenate([a, b], axis=1)
                            for a, b in zip(halves(moved), halves(other))
                        ],
                        axis=0,
                    ),
                    preferred_element_type=f32,
                )
                turned = jnp.where(strict, turned[:, :CH], 0.0) + turned[:, CH:]
            else:
                gk = gk + mm_t(left(tail_update), right_t(carry))
                other = pushed * tail_update
                r1 = jnp.dot(upper2, jnp.concatenate(halves(moved), axis=0), preferred_element_type=f32)
                r2 = jnp.dot(lower2, jnp.concatenate(halves(other), axis=0), preferred_element_type=f32)
                turned = jnp.where(strict, r1, 0.0) + r2
            grads_g[c] = jnp.sum(turned, -1, keepdims=True)
            grads_q[c] = gq
            grads_k[c] = gk
        grad_decays.append(jnp.concatenate(grads_g, axis=0))
        grad_strengths.append(jnp.concatenate(grads_b, axis=0))
        gq = jnp.concatenate(grads_q, axis=0)
        gk = jnp.concatenate(grads_k, axis=0)
        gv = jnp.concatenate(grads_v, axis=0)
        unit = parts[0] * q_norm
        gq = (CH ** (-0.5)) * q_norm * (gq - unit * jnp.sum(gq * unit, -1, keepdims=True))
        gk = k_norm * (gk - keys * jnp.sum(gk * keys, -1, keepdims=True))
        for index, g in enumerate((gq, gk, gv)):
            pre = pres[index]
            sig = sigmoid(pre)
            g = g * sig * (1.0 + pre * (1.0 - sig))
            gx, gw = conv_back(pre_ref[:, piece(index, h)], g, conv_ref[index][:, at], long_row)
            gpre_ref[:, piece(index, h)] = gx.astype(bf16)
            gwide_ref[0, TAPS * index : TAPS * (index + 1), at] = gw
        gwide_ref[0, 3 * TAPS : 3 * TAPS + 1, at] = norm_gain_sum
    lane = lax.broadcasted_iota(jnp.int32, (SEQ, CH), 1)
    gd = jnp.zeros((SEQ, CH), f32)
    gs = jnp.zeros((SEQ, CH), f32)
    for h in range(heads):
        gd = jnp.where(lane == h, grad_decays[h], gd)
        gs = jnp.where(lane == heads + h, grad_strengths[h], gs)
    sig = sigmoid(ab)
    grad_shift = gd[:, :heads] * rate * sigmoid(shift)
    gab = gs * sig * (1.0 - sig)
    for h in range(heads):
        gab = jnp.where(lane == h, grad_shift[:, h : h + 1], gab)
    gpre_ref[:, 4 * inner :] = gab.astype(bf16)
    gdecay_ref[0, 0:1, :] = jnp.sum(gd[:, :heads] * decay_all, 0, keepdims=True)
    gdecay_ref[0, 1:2, :] = jnp.sum(grad_shift, 0, keepdims=True)


def row_spec(width):
    return pl.BlockSpec((SEQ, width), lambda i: (i, 0))


def whole_spec(shape):
    return pl.BlockSpec(shape, lambda i: (0,) * len(shape))


def seq_spec(shape):
    return pl.BlockSpec((1,) + shape, lambda i: (i, 0, 0))


def mixer_forward(pre, conv_weight, decay, gain):
    rows = pre.shape[0]
    heads = decay.shape[1]
    width = heads * CH
    wide = jax.ShapeDtypeStruct((rows, width), f32)
    return pl.pallas_call(
        forward_kernel,
        grid=(rows // SEQ,),
        in_specs=[row_spec(pre.shape[1])]
        + [whole_spec(conv_weight.shape), whole_spec(decay.shape), whole_spec(gain.shape)],
        out_specs=[row_spec(width)] * 4,
        out_shape=[jax.ShapeDtypeStruct((rows, width), bf16), wide, wide, wide],
        compiler_params=pltpu.CompilerParams(vmem_limit_bytes=56 * 2**20),
        cost_estimate=pl.CostEstimate(flops=10**10, bytes_accessed=10**7, transcendentals=0),
        name="mixer_forward",
    )(pre, conv_weight, decay, gain)


def mixer_backward(pre, conv_weight, decay, gain, inverse, update, delta, grad):
    rows = pre.shape[0]
    heads = decay.shape[1]
    width = heads * CH
    count = rows // SEQ
    return pl.pallas_call(
        backward_kernel,
        grid=(count,),
        in_specs=[row_spec(pre.shape[1])]
        + [whole_spec(conv_weight.shape), whole_spec(decay.shape), whole_spec(gain.shape)]
        + [row_spec(width)] * 4,
        out_specs=[row_spec(pre.shape[1]), seq_spec((16, width)), seq_spec((2, heads))],
        out_shape=[
            jax.ShapeDtypeStruct(pre.shape, bf16),
            jax.ShapeDtypeStruct((count, 16, width), f32),
            jax.ShapeDtypeStruct((count, 2, heads), f32),
        ],
        compiler_params=pltpu.CompilerParams(vmem_limit_bytes=56 * 2**20),
        cost_estimate=pl.CostEstimate(flops=2 * 10**10, bytes_accessed=2 * 10**7, transcendentals=0),
        name="mixer_backward",
    )(pre, conv_weight, decay, gain, inverse, update, delta, grad)


def matmul(former, latter, kind=f32):
    return jnp.dot(former, latter, preferred_element_type=f32).astype(kind)


def matmul_rows(former, latter, kind=f32):
    return lax.dot_general(
        former, latter, (((0,), (0,)), ((), ())), preferred_element_type=f32
    ).astype(kind)


def matmul_back(former, latter, kind=f32):
    return lax.dot_general(
        former, latter, (((1,), (1,)), ((), ())), preferred_element_type=f32
    ).astype(kind)


def line_gather(own, axis, count, me):
    rightward, leftward = [own], [own]
    for step in range(1, count):
        rightward.append(
            lax.ppermute(rightward[-1], axis, [(d, d + 1) for d in range(step - 1, count - 1)])
        )
        leftward.append(
            lax.ppermute(leftward[-1], axis, [(d + 1, d) for d in range(count - step)])
        )
    blocks = []
    for block in range(count):
        chosen = own
        for device in range(count):
            if device > block:
                chosen = jnp.where(me == device, rightward[device - block], chosen)
            elif device < block:
                chosen = jnp.where(me == device, leftward[block - device], chosen)
        blocks.append(chosen)
    return blocks


def line_scatter(partial, axis, count, me):
    width = partial.shape[1] // count

    def block(index):
        at = jnp.clip(index, 0, count - 1) * width
        return lax.dynamic_slice_in_dim(partial, at, width, axis=1)

    rightward = leftward = None
    for step in range(1, count):
        send_right = block(count - step + me)
        send_left = block(step - count + me)
        if rightward is not None:
            send_right = (send_right.astype(f32) + rightward.astype(f32)).astype(bf16)
            send_left = (send_left.astype(f32) + leftward.astype(f32)).astype(bf16)
        rightward = lax.ppermute(send_right, axis, [(d, d + 1) for d in range(step)])
        leftward = lax.ppermute(
            send_left, axis, [(count - 1 - d, count - 2 - d) for d in range(step)]
        )
    total = block(me).astype(f32)
    return total + rightward.astype(f32) + leftward.astype(f32)


def sum_around(own, axis, count):
    total = own
    for step in range(1, count):
        total = total + lax.ppermute(own, axis, [(d, (d + step) % count) for d in range(count)])
    return total


def sum_doubling(own, axis, count):
    step = 1
    while step < count:
        own = own + lax.ppermute(own, axis, [(d, d ^ step) for d in range(count)])
        step *= 2
    return own


def body(
    block_input, cotangent, seq_count, attn_gain, w_query, w_key, w_value, w_gate,
    w_alpha, w_beta, conv_weight, decay_base, decay_bias, norm_gain, w_out, mlp_gain,
    w_mlp_gate, w_mlp_up, w_down, *, heads_count, groups_count,
):
    micro_count, row_count, width = block_input.shape
    me = lax.axis_index("head")
    features = heads_count * width
    heads = decay_base.shape[0]
    hidden_units = w_down.shape[0]
    inner = w_query.shape[1]
    pad = jnp.zeros((features, CH - 2 * heads), bf16)
    w_in = jnp.concatenate([w_query, w_key, w_value, w_gate, w_alpha, w_beta, pad], axis=1)
    w_up2 = jnp.concatenate([w_mlp_gate, w_mlp_up], axis=1)
    decay = jnp.stack([decay_base, decay_bias])
    gain_row = norm_gain[None]

    def gathered(own):
        return jnp.concatenate(line_gather(own, "head", heads_count, me), axis=1)

    def own_of(values):
        return lax.dynamic_slice_in_dim(values, me * width, width, axis=values.ndim - 1)

    with_gains = jnp.concatenate(
        [block_input[0], jnp.stack([attn_gain, mlp_gain]), jnp.zeros((14, width), bf16)], axis=0
    )
    sent = [with_gains] + [block_input[m] for m in range(1, micro_count)]
    attn_own = attn_gain.astype(f32)
    mlp_own = mlp_gain.astype(f32)

    raw = [gathered(x) for x in sent]
    attn_scale = raw[0][row_count].astype(f32)
    mlp_scale = raw[0][row_count + 1].astype(f32)
    steps = range(micro_count)
    st = [dict() for _ in steps]
    for m in steps:
        s = st[m]
        live = (jnp.arange(row_count) // SEQ < seq_count[m, 0])[:, None]
        low = jnp.where(live, raw[m][:row_count], jnp.zeros((), bf16))
        inputs = low.astype(f32)
        s["inputs_own"] = jnp.where(live, block_input[m], jnp.zeros((), bf16)).astype(f32)
        s["scale_in"] = lax.rsqrt(jnp.mean(inputs * inputs, -1, keepdims=True) + epsilon)
        s["normed"] = (inputs * s["scale_in"] * attn_scale).astype(bf16)
        s["pre"] = matmul(s["normed"], w_in)
        s["grad_output"] = jnp.where(live, cotangent[m], jnp.zeros((), bf16))
        s["mixed"], *s["saved"] = mixer_forward(s["pre"], conv_weight, decay, gain_row)
        attended = line_scatter(matmul(s["mixed"], w_out, bf16), "head", heads_count, me)
        s["hidden_own"] = s["inputs_own"] + attended
        s["hidden"] = gathered(s["hidden_own"].astype(bf16))
    for m in steps:
        s = st[m]
        hidden = s["hidden"].astype(f32)
        s["scale_mid"] = lax.rsqrt(jnp.mean(hidden * hidden, -1, keepdims=True) + epsilon)
        s["normed_mid"] = (hidden * s["scale_mid"] * mlp_scale).astype(bf16)
        acts = matmul(s["normed_mid"], w_up2)
        gate_act, up_act = acts[:, :hidden_units], acts[:, hidden_units:]
        sig = jax.nn.sigmoid(gate_act)
        silu = gate_act * sig
        s["product"] = (silu * up_act).astype(bf16)
        grad_product = matmul_back(s["grad_output"], w_down)
        grad_gate = (grad_product * up_act * sig * (1.0 + gate_act * (1.0 - sig))).astype(bf16)
        grad_up = (grad_product * silu).astype(bf16)
        s["grad_acts"] = jnp.concatenate([grad_gate, grad_up], axis=1)
        s["grad_mid_own"] = line_scatter(
            matmul_back(s["grad_acts"], w_up2, bf16), "head", heads_count, me
        )
        s["grad_mid"] = gathered(s["grad_mid_own"].astype(bf16))
        s["output"] = (
            s["hidden_own"]
            + line_scatter(matmul(s["product"], w_down, bf16), "head", heads_count, me)
        ).astype(bf16)

    def rows_of(name):
        return jnp.concatenate([st[m][name] for m in steps], axis=0)

    def scattered(values, dimension):
        return lax.psum_scatter(values, "dp", scatter_dimension=dimension, tiled=True).astype(f32)

    up2_grad = scattered(matmul_rows(rows_of("normed_mid"), rows_of("grad_acts"), bf16), 0)
    down_grad = scattered(matmul_rows(rows_of("product"), rows_of("grad_output"), bf16), 1)
    mlp_gain_grad = sum(
        jnp.sum(s["grad_mid_own"] * s["hidden_own"] * s["scale_mid"], 0) for s in st
    )
    for m in steps:
        s = st[m]
        hidden = s["hidden"].astype(f32)
        grad_mid = s["grad_mid"].astype(f32)
        scale_mid = s["scale_mid"]
        dot_mid = jnp.sum(grad_mid * mlp_scale * hidden, -1, keepdims=True)
        back = scale_mid**3 * dot_mid / features
        s["grad_low"] = (
            s["grad_output"].astype(f32) + scale_mid * mlp_scale * grad_mid - hidden * back
        ).astype(bf16)
        s["grad_hidden_own"] = (
            own_of(s["grad_output"]).astype(f32)
            + scale_mid * mlp_own * s["grad_mid_own"]
            - s["hidden_own"] * back
        )
        grad_mixed = matmul_back(s["grad_low"], w_out)
        s["grad_pre"], wide, s["decay_sums"] = mixer_backward(
            s["pre"], conv_weight, decay, gain_row, *s["saved"], grad_mixed
        )
        s["wide"] = wide
    out_grad = scattered(matmul_rows(rows_of("mixed"), rows_of("grad_low"), bf16), 1)
    in_grad = scattered(matmul_rows(rows_of("normed"), rows_of("grad_pre"), bf16), 0)
    input_grads = []
    attn_gain_grad = 0.0
    for m in steps:
        s = st[m]
        dot_in = sum_around(
            jnp.sum(s["grad_pre"].astype(f32) * s["pre"], -1) / s["scale_in"][:, 0],
            "head",
            heads_count,
        )[:, None]
        grad_in = line_scatter(matmul_back(s["grad_pre"], w_in, bf16), "head", heads_count, me)
        scale_in = s["scale_in"]
        input_grads.append(
            s["grad_hidden_own"]
            + scale_in * attn_own * grad_in
            - s["inputs_own"] * scale_in**3 * dot_in / features
        )
        attn_gain_grad = attn_gain_grad + jnp.sum(grad_in * s["inputs_own"] * scale_in, 0)
    wide = sum(jnp.sum(s["wide"], 0) for s in st)
    decays = sum(jnp.sum(s["decay_sums"], 0) for s in st)
    taps = 3 * TAPS
    norm_sum = jnp.sum(wide[taps].reshape(heads, CH), 0)
    norm_sum = sum_around(norm_sum, "head", heads_count)
    small = jnp.concatenate(
        [
            wide[:taps].reshape(-1), attn_gain_grad, mlp_gain_grad,
            jnp.pad(norm_sum, (0, inner - CH)),
            jnp.pad(decays.reshape(-1), (0, inner - 2 * heads)),
        ]
    ).reshape(-1, CH)
    small = sum_doubling(small, "dp", groups_count).reshape(-1)
    at = taps * inner
    return (
        jnp.stack([s["output"] for s in st]),
        jnp.stack(input_grads),
        small[at : at + width],
        in_grad[:, :inner],
        in_grad[:, inner : 2 * inner],
        in_grad[:, 2 * inner : 3 * inner],
        in_grad[:, 3 * inner : 4 * inner],
        in_grad[:, 4 * inner : 4 * inner + heads],
        in_grad[:, 4 * inner + heads : 4 * inner + 2 * heads],
        small[:at].reshape(3, TAPS, inner),
        small[at + 2 * width + inner : at + 2 * width + inner + heads],
        small[at + 2 * width + inner + heads : at + 2 * width + inner + 2 * heads],
        small[at + 2 * width : at + 2 * width + CH],
        out_grad,
        small[at + width : at + 2 * width],
        up2_grad[:, :hidden_units],
        up2_grad[:, hidden_units:],
        down_grad,
    )


def solution(mesh):
    return jax.shard_map(
        functools.partial(
            body, heads_count=mesh.shape["head"], groups_count=mesh.shape["dp"]
        ),
        mesh=mesh,
        in_specs=(
            P(None, "dp", "head"), P(None, "dp", None), P(None, "dp"), P("head"),
            P(None, "head"), P(None, "head"), P(None, "head"), P(None, "head"),
            P(None, "head"), P(None, "head"), P(None, None, "head"), P("head"), P("head"),
            P(), P("head", None), P("head"), P(None, "head"), P(None, "head"), P("head", None),
        ),
        out_specs=(
            P(None, "dp", "head"), P(None, "dp", "head"), P("head"),
            P("dp", "head"), P("dp", "head"), P("dp", "head"), P("dp", "head"),
            P("dp", "head"), P("dp", "head"), P(None, None, "head"), P("head"), P("head"),
            P(), P("head", "dp"), P("head"), P("dp", "head"), P("dp", "head"), P("head", "dp"),
        ),
        check_vma=False,
    )
```

```python
import functools
import jax
import jax.numpy as jnp
from jax import lax
from jax.experimental import pallas as pl
from jax.experimental.pallas import tpu as pltpu
from jax.experimental.layout import Layout, with_layout_constraint
from jax.sharding import PartitionSpec as P

SEQ = 256
CH = 128
TAPS = 4
epsilon = 1e-06
f32 = jnp.float32
bf16 = jnp.bfloat16


def halves(x):
    high = x.astype(bf16)
    return high, (x - high.astype(f32)).astype(bf16)


def left(x):
    return jnp.concatenate(halves(x), axis=1)


def right(x):
    row = jnp.concatenate(halves(x), axis=1)
    return jnp.concatenate([row, row], axis=0)


def right_t(x):
    high, low = halves(x)
    return jnp.concatenate(
        [jnp.concatenate([high, high], axis=1), jnp.concatenate([low, low], axis=1)], axis=0
    )


def fold(r):
    return r[:, :CH] + r[:, CH:]


def mm(l, r):
    return fold(jnp.dot(l, r, preferred_element_type=f32))


def mm_t(l, r):
    return fold(lax.dot_general(l, r, (((1,), (1,)), ((), ())), preferred_element_type=f32))


def grids():
    row = lax.broadcasted_iota(jnp.int32, (CH, CH), 0)
    col = lax.broadcasted_iota(jnp.int32, (CH, CH), 1)
    return row, col


def sum_matrix(row, col):
    lower = (row >= col).astype(bf16)
    zero = jnp.zeros((CH, CH), bf16)
    return jnp.concatenate(
        [
            jnp.concatenate([lower, jnp.full((CH, CH), -1, bf16)], axis=1),
            jnp.concatenate([lower, zero], axis=1),
            jnp.concatenate([(row < col).astype(bf16), zero], axis=1),
        ],
        axis=0,
    )


def decay_sums(decay, row, col, sums):
    wide = jnp.broadcast_to(decay, (CH, CH))
    cut = jnp.where(row <= col, wide, 0.0)
    r = jnp.concatenate(
        [jnp.concatenate(halves(wide), axis=1), jnp.concatenate(halves(cut), axis=1)], axis=0
    )
    out = fold(jnp.dot(sums, r, preferred_element_type=f32))
    return out[:CH], out[CH : 2 * CH], out[2 * CH :]


def shifted(x, by, row):
    if by == 0:
        return x
    return jnp.where(row >= by, pltpu.roll(x, by, 0), 0.0)


def shifted_back(x, by, row):
    if by == 0:
        return x
    return jnp.where(row < SEQ - by, pltpu.roll(x, SEQ - by, 0), 0.0)


def sigmoid(x):
    return 0.5 + 0.5 * jnp.tanh(0.5 * x)


def conv_sum(x, taps, row):
    total = x * taps[TAPS - 1 : TAPS]
    for by in range(1, TAPS):
        total = total + shifted(x, by, row) * taps[TAPS - 1 - by : TAPS - by]
    return total


def conv_back(x, grad, taps, row):
    grad_x = grad * taps[TAPS - 1 : TAPS]
    sums = [jnp.sum(grad * x, 0, keepdims=True)]
    for by in range(1, TAPS):
        moved = shifted_back(grad, by, row)
        grad_x = grad_x + moved * taps[TAPS - 1 - by : TAPS - by]
        sums.append(jnp.sum(moved * x, 0, keepdims=True))
    return grad_x, jnp.concatenate(sums[::-1], axis=0)


def norm_of(x):
    return lax.rsqrt(jnp.sum(x * x, -1, keepdims=True) + epsilon)


def softplus(x):
    return jnp.maximum(x, 0.0) + jnp.log(1.0 + jnp.exp(-jnp.abs(x)))


def take_turns(workers):
    while workers:
        workers = [worker for worker in workers if next(worker, workers) is None]


def forward_kernel(
    pre_ref, conv_ref, decay_ref, gain_ref,
    mixed_ref, inverse_ref, update_ref, delta_ref,
):
    heads = decay_ref.shape[1]
    inner = heads * CH

    def piece(index, h):
        return slice(index * inner + h * CH, index * inner + (h + 1) * CH)

    row, col = grids()
    long_row = lax.broadcasted_iota(jnp.int32, (SEQ, CH), 0)
    sums = sum_matrix(row, col)
    within = row >= col
    eye = (row == col).astype(f32)
    ab = pre_ref[:, 4 * inner :]
    decay_all = -jnp.exp(decay_ref[0:1, :]) * softplus(ab[:, :heads] + decay_ref[1:2, :])
    strength_all = sigmoid(ab[:, heads : 2 * heads])
    systems, inverses, kept = [None] * 2 * heads, [None] * 2 * heads, [None] * 2 * heads

    def prepare(h):
        at = slice(h * CH, (h + 1) * CH)
        parts = []
        for index in range(3):
            pre = conv_sum(pre_ref[:, piece(index, h)], conv_ref[index][:, at], long_row)
            parts.append(pre * sigmoid(pre))
        queries = parts[0] * norm_of(parts[0]) * CH ** (-0.5)
        keys = parts[1] * norm_of(parts[1])
        yield
        for c in range(2):
            span = slice(c * CH, (c + 1) * CH)
            q, k, v = queries[span], keys[span], parts[2][span]
            spread, start, tail = decay_sums(decay_all[span, h : h + 1], row, col, sums)
            falloff = jnp.where(within, jnp.exp(jnp.minimum(spread, 0.0)), 0.0)
            k_left = left(k)
            both = mm_t(jnp.concatenate([k_left, left(q)], axis=0), right_t(k))
            yield
            beta = jnp.broadcast_to(strength_all[span, h : h + 1], (CH, CH))
            system = jnp.where(row > col, beta * falloff * both[:CH], 0.0)
            systems[2 * h + c] = system
            inverses[2 * h + c] = eye - jnp.where(
                (row // 2 == col // 2) & (row % 2 > col % 2), system, 0.0
            )
            kept[2 * h + c] = (
                q, k_left, v, k, beta, falloff * both[CH:], jnp.exp(start), jnp.exp(tail)
            )

    take_turns([prepare(h) for h in range(heads)])
    size = 2
    while size < CH:
        mask = (row // (2 * size) == col // (2 * size)) & ((row // size) % 2 > (col // size) % 2)
        steps = [
            mm(left(inverse), right(jnp.where(mask, system, 0.0)))
            for inverse, system in zip(inverses, systems)
        ]
        inverses = [
            inverse - mm(left(step), right(inverse)) for inverse, step in zip(inverses, steps)
        ]
        size *= 2

    def solve(h):
        at = slice(h * CH, (h + 1) * CH)
        q, k_left, v, k, beta, scores, start, tail = kept[2 * h]
        first_update = mm(left(inverses[2 * h]), right(beta * v))
        yield
        first_out = mm(left(scores), right(first_update))
        yield
        state = mm(left(k.T), right(tail * first_update))
        yield
        q, k_left, v, k, beta, scores, start, tail = kept[2 * h + 1]
        read = mm(jnp.concatenate([k_left, left(q)], axis=0), right(state))
        yield
        second_update = mm(left(inverses[2 * h + 1]), right(beta * (v - start * read[:CH])))
        yield
        second_out = start * read[CH:] + mm(left(scores), right(second_update))
        yield
        for c, (update, out) in enumerate(((first_update, first_out), (second_update, second_out))):
            span = slice(c * CH, (c + 1) * CH)
            update_ref[span, at] = update
            delta_ref[span, at] = out
            inverse_ref[span, at] = inverses[2 * h + c].T
            scale = lax.rsqrt(jnp.mean(out * out, -1, keepdims=True) + epsilon)
            gate = pre_ref[span, piece(3, h)]
            mixed_ref[span, at] = (
                out * scale * gain_ref[...] * (gate * sigmoid(gate))
            ).astype(bf16)

    take_turns([solve(h) for h in range(heads)])


def backward_kernel(
    pre_ref, conv_ref, decay_ref, gain_ref,
    inverse_ref, update_ref, delta_ref, grad_ref,
    gpre_ref, gwide_ref, gdecay_ref, gdot_ref,
):
    heads = decay_ref.shape[1]
    inner = heads * CH

    def piece(index, h):
        return slice(index * inner + h * CH, index * inner + (h + 1) * CH)

    row, col = grids()
    long_row = lax.broadcasted_iota(jnp.int32, (SEQ, CH), 0)
    sums = sum_matrix(row, col)
    within = row >= col
    strict = row > col
    upper = (row <= col).astype(bf16)
    upper2 = jnp.concatenate([upper, upper], axis=1)
    lower = strict.astype(bf16)
    lower2 = jnp.concatenate([lower, lower], axis=1)
    ab = pre_ref[:, 4 * inner :]
    rate = -jnp.exp(decay_ref[0:1, :])
    shift = ab[:, :heads] + decay_ref[1:2, :]
    decay_all = rate * softplus(shift)
    strength_all = sigmoid(ab[:, heads : 2 * heads])
    grad_decays, grad_strengths, dots = [None] * heads, [None] * heads, [None] * heads

    def one_head(h):
        at = slice(h * CH, (h + 1) * CH)
        pres, parts = [], []
        for index in range(3):
            pre = conv_sum(pre_ref[:, piece(index, h)], conv_ref[index][:, at], long_row)
            pres.append(pre)
            parts.append(pre * sigmoid(pre))
        q_norm, k_norm = norm_of(parts[0]), norm_of(parts[1])
        queries = parts[0] * q_norm * CH ** (-0.5)
        keys = parts[1] * k_norm
        yield
        out = delta_ref[:, at]
        gate = pre_ref[:, piece(3, h)]
        grad = grad_ref[:, at]
        gain = gain_ref[...]
        scale = lax.rsqrt(jnp.mean(out * out, -1, keepdims=True) + epsilon)
        sig = sigmoid(gate)
        scaled = out * scale
        grad_gate = grad * scaled * gain * sig * (1.0 + gate * (1.0 - sig))
        gpre_ref[:, piece(3, h)] = grad_gate.astype(bf16)
        dots[h] = grad_gate * gate
        grad_normed = grad * gate * sig
        norm_gain_sum = jnp.sum(grad_normed * scaled, 0, keepdims=True)
        grad_scaled = grad_normed * gain
        grad_out = scale * (
            grad_scaled - scaled * jnp.mean(grad_scaled * scaled, -1, keepdims=True)
        )
        yield
        stuff = []
        for c in range(2):
            span = slice(c * CH, (c + 1) * CH)
            q, k, v = queries[span], keys[span], parts[2][span]
            spread, start, tail = decay_sums(decay_all[span, h : h + 1], row, col, sums)
            falloff = jnp.where(within, jnp.exp(jnp.minimum(spread, 0.0)), 0.0)
            q_left, k_left = left(q), left(k)
            both = mm_t(jnp.concatenate([k_left, q_left], axis=0), right_t(k))
            yield
            beta = jnp.broadcast_to(strength_all[span, h : h + 1], (CH, CH))
            stuff.append(
                (q, k, v, falloff, both[:CH] * falloff, both[CH:] * falloff, beta,
                 jnp.exp(start), jnp.exp(tail), q_left, k_left)
            )
        carry = None
        grads_q, grads_k, grads_v, grads_g, grads_b = [None] * 2, [None] * 2, [None] * 2, [None] * 2, [None] * 2
        first_update = update_ref[0:CH, at]
        tail_update = stuff[0][8] * first_update
        state = mm(left(stuff[0][1].T), right(tail_update))
        yield
        for c in (1, 0):
            span = slice(c * CH, (c + 1) * CH)
            q, k, v, falloff, similar, scores, beta, start, tail, q_left, k_left = stuff[c]
            update = update_ref[span, at]
            go = grad_out[span]
            grad_update = mm(left(scores.T), right(go))
            yield
            target = v
            if c == 1:
                read = mm(jnp.concatenate([k_left, q_left], axis=0), right(state))
                yield
                target = v - start * read[:CH]
            else:
                pushed = mm(k_left, right(carry))
                yield
                grad_update = grad_update + tail * pushed
            grad_write = mm(left(inverse_ref[span, at]), right(grad_update))
            yield
            outer = mm_t(
                jnp.concatenate([left(grad_write), left(go)], axis=0), right_t(update)
            )
            yield
            grad_system = jnp.where(strict, -outer[:CH], 0.0)
            grad_scores = jnp.where(within, outer[CH:], 0.0)
            grads_b[c] = jnp.sum(grad_write * target + grad_system * similar, -1, keepdims=True)
            grad_target = beta * grad_write
            grads_v[c] = grad_target
            grad_similar = grad_system * beta * falloff
            grad_dots = grad_scores * falloff
            moved = grad_system * beta * similar + grad_scores * scores
            k_right = right(k)
            back = mm(
                jnp.concatenate(
                    [left(grad_dots), left(grad_similar + grad_similar.T)], axis=0
                ),
                k_right,
            )
            yield
            gq = back[:CH]
            gk = back[CH:] + mm(left(grad_dots.T), right(q))
            yield
            if c == 1:
                through_out, through_read = start * go, -start * grad_target
                more = mm_t(
                    jnp.concatenate([left(through_out), left(through_read)], axis=0),
                    right_t(state),
                )
                yield
                gq = gq + more[:CH]
                gk = gk + more[CH:]
                carry = mm(left(q.T), right(through_out)) + mm(left(k.T), right(through_read))
                yield
                other = through_out * read[CH:] + through_read * read[:CH]
                turned = jnp.dot(
                    upper2,
                    jnp.concatenate(
                        [
                            jnp.concatenate([a, b], axis=1)
                            for a, b in zip(halves(moved), halves(other))
                        ],
                        axis=0,
                    ),
                    preferred_element_type=f32,
                )
                turned = jnp.where(strict, turned[:, :CH], 0.0) + turned[:, CH:]
            else:
                gk = gk + mm_t(left(tail_update), right_t(carry))
                yield
                other = pushed * tail_update
                r1 = jnp.dot(upper2, jnp.concatenate(halves(moved), axis=0), preferred_element_type=f32)
                r2 = jnp.dot(lower2, jnp.concatenate(halves(other), axis=0), preferred_element_type=f32)
                turned = jnp.where(strict, r1, 0.0) + r2
            grads_g[c] = jnp.sum(turned, -1, keepdims=True)
            grads_q[c] = gq
            grads_k[c] = gk
        grad_decays[h] = jnp.concatenate(grads_g, axis=0)
        grad_strengths[h] = jnp.concatenate(grads_b, axis=0)
        gq = jnp.concatenate(grads_q, axis=0)
        gk = jnp.concatenate(grads_k, axis=0)
        gv = jnp.concatenate(grads_v, axis=0)
        yield
        unit = parts[0] * q_norm
        gq = (CH ** (-0.5)) * q_norm * (gq - unit * jnp.sum(gq * unit, -1, keepdims=True))
        gk = k_norm * (gk - keys * jnp.sum(gk * keys, -1, keepdims=True))
        for index, g in enumerate((gq, gk, gv)):
            pre = pres[index]
            sig = sigmoid(pre)
            g = g * sig * (1.0 + pre * (1.0 - sig))
            gx, gw = conv_back(pre_ref[:, piece(index, h)], g, conv_ref[index][:, at], long_row)
            gpre_ref[:, piece(index, h)] = gx.astype(bf16)
            dots[h] = dots[h] + gx * pre_ref[:, piece(index, h)]
            gwide_ref[0, TAPS * index : TAPS * (index + 1), at] = gw
        gwide_ref[0, 3 * TAPS : 3 * TAPS + 1, at] = norm_gain_sum

    take_turns([one_head(h) for h in range(heads)])
    lane = lax.broadcasted_iota(jnp.int32, (SEQ, CH), 1)
    gd = jnp.zeros((SEQ, CH), f32)
    gs = jnp.zeros((SEQ, CH), f32)
    for h in range(heads):
        gd = jnp.where(lane == h, grad_decays[h], gd)
        gs = jnp.where(lane == heads + h, grad_strengths[h], gs)
    sig = sigmoid(ab)
    grad_shift = gd[:, :heads] * rate * sigmoid(shift)
    gab = gs * sig * (1.0 - sig)
    for h in range(heads):
        gab = jnp.where(lane == h, grad_shift[:, h : h + 1], gab)
    gpre_ref[:, 4 * inner :] = gab.astype(bf16)
    total = jnp.where(lane < 2 * heads, gab * ab, 0.0)
    for h in range(heads):
        total = total + dots[h]
    gdot_ref[...] = jnp.sum(total, -1, keepdims=True)
    gdecay_ref[0, 0:1, :] = jnp.sum(gd[:, :heads] * decay_all, 0, keepdims=True)
    gdecay_ref[0, 1:2, :] = jnp.sum(grad_shift, 0, keepdims=True)


def row_spec(width):
    return pl.BlockSpec((SEQ, width), lambda i: (i, 0))


def whole_spec(shape):
    return pl.BlockSpec(shape, lambda i: (0,) * len(shape))


def seq_spec(shape):
    return pl.BlockSpec((1,) + shape, lambda i: (i, 0, 0))


def mixer_forward(pre, conv_weight, decay, gain):
    rows = pre.shape[0]
    heads = decay.shape[1]
    width = heads * CH
    wide = jax.ShapeDtypeStruct((rows, width), f32)
    return pl.pallas_call(
        forward_kernel,
        grid=(rows // SEQ,),
        in_specs=[row_spec(pre.shape[1])]
        + [whole_spec(conv_weight.shape), whole_spec(decay.shape), whole_spec(gain.shape)],
        out_specs=[row_spec(width)] * 4,
        out_shape=[jax.ShapeDtypeStruct((rows, width), bf16), wide, wide, wide],
        compiler_params=pltpu.CompilerParams(vmem_limit_bytes=56 * 2**20),
        cost_estimate=pl.CostEstimate(flops=10**10, bytes_accessed=10**7, transcendentals=0),
        name="mixer_forward",
    )(pre, conv_weight, decay, gain)


def mixer_backward(pre, conv_weight, decay, gain, inverse, update, delta, grad, sequence, shared, slot, slots):
    heads = decay.shape[1]
    width = heads * CH

    def rows(columns):
        return pl.BlockSpec((SEQ, columns), lambda i: (sequence, 0))

    def kernel(*refs):
        backward_kernel(*refs[:8], *refs[-4:])

    operands = [pre, conv_weight, decay, gain, inverse, update, delta, grad]
    in_specs = (
        [rows(pre.shape[1])]
        + [whole_spec(x.shape) for x in (conv_weight, decay, gain)]
        + [rows(width)] * 4
    )
    if shared is not None:
        operands.append(shared)
        in_specs.append(pl.BlockSpec(memory_space=pl.ANY))
    return pl.pallas_call(
        kernel,
        grid=(1,),
        in_specs=in_specs,
        out_specs=[
            pl.BlockSpec((SEQ, pre.shape[1]), lambda i: (slot, 0)),
            seq_spec((16, width)),
            seq_spec((2, heads)),
            pl.BlockSpec((SEQ, 1), lambda i: (0, 0)),
        ],
        out_shape=[
            jax.ShapeDtypeStruct((slots * SEQ, pre.shape[1]), bf16),
            jax.ShapeDtypeStruct((1, 16, width), f32),
            jax.ShapeDtypeStruct((1, 2, heads), f32),
            jax.ShapeDtypeStruct((SEQ, 1), f32),
        ],
        input_output_aliases={} if shared is None else {8: 0},
        compiler_params=pltpu.CompilerParams(vmem_limit_bytes=56 * 2**20),
        cost_estimate=pl.CostEstimate(flops=10**10, bytes_accessed=10**7, transcendentals=0),
        name="mixer_backward",
    )(*operands)


HEAD = "head"
DP = "dp"


def matmul(former, latter, kind=f32):
    return jnp.dot(former, latter, preferred_element_type=f32).astype(kind)


def matmul_rows(former, latter, kind=f32):
    return lax.dot_general(
        former, latter, (((0,), (0,)), ((), ())), preferred_element_type=f32
    ).astype(kind)


def matmul_back(former, latter, kind=f32):
    return lax.dot_general(
        former, latter, (((1,), (1,)), ((), ())), preferred_element_type=f32
    ).astype(kind)


def row_major(x):
    return with_layout_constraint(x, Layout(major_to_minor=tuple(range(x.ndim))))


def ring_order(count):
    return [0] + list(range(1, count, 2)) + [d for d in range(count - 1, 0, -1) if d % 2 == 0]


class Bag:
    pass


class Ring:
    def __init__(self, count):
        self.count = count
        self.order = ring_order(count)
        self.pairs = [(self.order[i], self.order[(i + 1) % count]) for i in range(count)]
        self.me = lax.axis_index(HEAD)
        self.place = self.lookup([self.order.index(d) for d in range(count)], self.me)
        self.bags = []
        self.transfers = []

    def lookup(self, table, index):
        found = jnp.int32(table[0])
        for i in range(1, self.count):
            found = jnp.where(index == i, table[i], found)
        return found

    def bag(self):
        self.bags.append(Bag())
        return self.bags[-1]

    def gather(self, own):
        return Gather(self, own)

    def scatter(self, partial):
        return Scatter(self, partial)

    def tick(self, *landing):
        for transfer in landing:
            transfer.land()
        state = [vars(bag) for bag in self.bags] + [t.state for t in self.transfers]
        flat, tree = jax.tree.flatten(state)
        state = jax.tree.unflatten(tree, lax.optimization_barrier(flat))
        for bag, values in zip(self.bags, state):
            vars(bag).update(values)
        for transfer, values in zip(self.transfers, state[len(self.bags) :]):
            transfer.state = values

    def hops(self, part):
        return [s for s in range(1, self.count) if (s - 1) * 3 // (self.count - 1) == part]

    def send(self, block):
        return lax.ppermute(block, HEAD, self.pairs)


class Gather:
    def __init__(self, ring, own):
        self.ring = ring
        self.state = [own]
        self.air = []
        self.part = 0
        ring.transfers.append(self)

    def hop(self):
        for _ in self.ring.hops(self.part):
            self.air.append(self.ring.send((self.state + self.air)[-1]))
        self.part += 1

    def land(self):
        self.state = self.state + self.air
        self.air = []

    def take(self):
        return jnp.concatenate(self.take_blocks(), axis=1)

    def take_blocks(self):
        self.ring.transfers.remove(self)
        return self.blocks()

    def blocks(self):
        ring = self.ring
        blocks = []
        for block in range(ring.count):
            chosen = self.state[0]
            at = ring.order.index(block)
            for device in range(ring.count):
                back = (ring.order.index(device) - at) % ring.count
                if back:
                    chosen = jnp.where(ring.me == device, self.state[back], chosen)
            blocks.append(chosen)
        return blocks


class Scatter:
    def __init__(self, ring, partial):
        self.ring = ring
        self.state = [partial]
        self.part = 0
        ring.transfers.append(self)

    def block(self, back):
        ring, partial = self.ring, self.state[0]
        width = partial.shape[1] // ring.count
        index = ring.lookup(ring.order, (ring.place + ring.count - back) % ring.count)
        return lax.dynamic_slice_in_dim(partial, index * width, width, axis=1)

    def hop(self):
        for step in self.ring.hops(self.part):
            send = self.block(step)
            if step > 1:
                send = (send.astype(f32) + self.state[1].astype(f32)).astype(bf16)
            self.state = [self.state[0], self.ring.send(send)]
        self.air = self.state.pop()
        self.part += 1

    def land(self):
        self.state = [self.state[0], self.air]

    def take(self):
        self.ring.transfers.remove(self)
        return self.block(0).astype(f32) + self.state[1].astype(f32)


class Cube:
    def __init__(self, total, cut, count, ring):
        self.count = count
        self.me = lax.axis_index(DP)
        bits = list(range(1, count.bit_length() - 1))
        self.halves = [total[:, :cut], total[:, cut:]]
        self.state = []
        self.todo = [bits, bits[::-1]]
        self.left = [list(bits), list(bits)]
        ring.transfers.append(self)

    def pick(self, x, todo, left, flip):
        blocks = 2 ** len(left)
        size = x.shape[0] // blocks
        at = 1 << left.index(todo[0])
        high = (((self.me >> todo[0]) & 1) ^ flip) == 1
        rows = [
            jnp.where(high, x[(i + at) * size : (i + at + 1) * size], x[i * size : (i + 1) * size])
            for i in range(blocks)
            if not i & at
        ]
        return jnp.concatenate(rows, axis=0)

    def hop(self):
        self.air = [
            lax.ppermute(
                self.pick(x, todo, left, 1), DP, [(d, d ^ (1 << todo[0])) for d in range(self.count)]
            )
            for x, todo, left in zip(self.halves, self.todo, self.left)
        ]

    def land(self):
        self.state = self.air

    def add(self):
        halves = []
        for i in range(2):
            x, todo, left, got = self.halves[i], self.todo[i], self.left[i], self.state[i]
            total = self.pick(x, todo, left, 0).astype(f32) + got.astype(f32)
            self.left[i] = [bit for bit in left if bit != todo[0]]
            self.todo[i] = todo[1:]
            halves.append(total.astype(bf16) if self.todo[i] else total)
        self.halves, self.state = halves, []


class Sums:
    def __init__(self, ring, own):
        self.state = [own]
        self.step = 1
        ring.transfers.append(self)

    def around(self, count):
        own = self.state[0]
        self.air = [
            lax.ppermute(own, HEAD, [(d, (d + step) % count) for d in range(count)])
            for step in range(1, count)
        ]

    def double(self, count, times):
        total = self.state[0]
        for _ in range(times):
            if self.step < count:
                total = total + lax.ppermute(total, DP, [(d, d ^ self.step) for d in range(count)])
                self.step *= 2
        self.state, self.air = [], [total]

    def land(self):
        self.state = [sum(self.state + self.air)]


def body(
    block_input, cotangent, seq_count, attn_gain, w_query, w_key, w_value, w_gate,
    w_alpha, w_beta, conv_weight, decay_base, decay_bias, norm_gain, w_out, mlp_gain,
    w_mlp_gate, w_mlp_up, w_down, *, heads_count, groups_count,
):
    micro_count, row_count, width = block_input.shape
    ring = Ring(heads_count)
    every, a, b = ring.bag(), ring.bag(), ring.bag()
    micros = (a, b)
    index = {a: 0, b: 1}
    features = heads_count * width
    heads = decay_base.shape[0]
    hidden_units = w_down.shape[0]
    inner = w_query.shape[1]
    per_micro = row_count // SEQ
    decay = jnp.stack([decay_base, decay_bias])
    gain_row = norm_gain[None]
    attn_own = attn_gain.astype(f32)
    mlp_own = mlp_gain.astype(f32)
    core = lax.axis_index(DP) & 1

    def own_of(values):
        return lax.dynamic_slice_in_dim(values, ring.me * width, width, axis=values.ndim - 1)

    def live_rows(m):
        return (jnp.arange(row_count) // SEQ < seq_count[index[m], 0])[:, None]

    def inputs_own(m):
        return jnp.where(live_rows(m), block_input[index[m]], jnp.zeros((), bf16)).astype(f32)

    def grad_output(m):
        return jnp.where(live_rows(m), cotangent[index[m]], jnp.zeros((), bf16))

    def normalise(m, raw):
        m.low = jnp.where(live_rows(m), raw, jnp.zeros((), bf16))
        inputs = m.low.astype(f32)
        m.scale_in = lax.rsqrt(jnp.mean(inputs * inputs, -1, keepdims=True) + epsilon)
        m.normed = (inputs * m.scale_in * every.gains[:1]).astype(bf16)

    def project(m):
        m.pre = matmul(m.normed, every.w_in)

    def mix(m):
        m.mixed, *m.saved = mixer_forward(m.pre, conv_weight, decay, gain_row)

    def attend(m, mixed):
        m.hidden = m.low.astype(f32) + matmul(mixed, every.w_out)

    def normalise_mid(m):
        hidden = m.hidden
        m.scale_mid = lax.rsqrt(jnp.mean(hidden * hidden, -1, keepdims=True) + epsilon)
        m.normed_mid = (hidden * m.scale_mid * every.gains[1:]).astype(bf16)

    def expand(m):
        m.acts = matmul(m.normed_mid, every.w_up2)

    def activate(m):
        gate_act, up_act = m.acts[:, :hidden_units], m.acts[:, hidden_units:]
        del m.acts
        sig = jax.nn.sigmoid(gate_act)
        silu = gate_act * sig
        m.product = (silu * up_act).astype(bf16)
        grad_product = matmul_back(grad_output(m), w_down)
        grad_gate = (grad_product * up_act * sig * (1.0 + gate_act * (1.0 - sig))).astype(bf16)
        grad_up = (grad_product * silu).astype(bf16)
        m.grad_acts = jnp.concatenate([grad_gate, grad_up], axis=1)

    def back_mid(m):
        m.part_mid = matmul_back(m.grad_acts, every.w_up2, bf16)

    def contract(m):
        m.part_out = matmul(m.product, w_down, bf16)

    def back_hidden(m, grad_mid):
        grad_mid = grad_mid.astype(f32)
        scale, gain = m.scale_mid, every.gains[1:]
        dot_mid = jnp.sum(grad_mid * gain * m.hidden, -1, keepdims=True)
        back = scale**3 * dot_mid / features
        out = grad_output(m)
        m.grad_low = (out.astype(f32) + scale * gain * grad_mid - m.hidden * back).astype(bf16)
        m.grad_hidden_own = (
            own_of(out).astype(f32) + scale * mlp_own * m.grad_mid_own - own_of(m.hidden) * back
        )
        m.grad_mixed = matmul_back(m.grad_low, w_out)

    def mix_back(m, sequence):
        slot = index[m] * per_micro + sequence
        every.grad_pre, wide, decays, dots = mixer_backward(
            m.pre, conv_weight, decay, gain_row, *m.saved, m.grad_mixed, sequence,
            every.grad_pre if slot else None, slot, micro_count * per_micro,
        )
        every.wide = every.wide + wide[0] if slot else wide[0]
        every.decays = every.decays + decays[0] if slot else decays[0]
        m.dots = (m.dots if sequence else []) + [dots[:, 0]]

    def back_in(m):
        grad_pre = every.grad_pre[index[m] * row_count : (index[m] + 1) * row_count]
        m.part_in = matmul_back(grad_pre, every.w_in, bf16)
        m.dot_in = jnp.concatenate(m.dots) / m.scale_in[:, 0]

    def gain_in(m):
        m.gain_in = jnp.sum(m.part_in.astype(f32) * m.low.astype(f32) * m.scale_in, 0)

    def finish_output(m, summed):
        m.output = (own_of(m.hidden) + summed).astype(bf16)

    def finish_input(m, grad_in, dot_in):
        m.input_grad = (
            m.grad_hidden_own
            + m.scale_in * attn_own * grad_in
            - inputs_own(m) * m.scale_in**3 * dot_in[:, None] / features
        )

    def rows_of(former, latter):
        return jnp.concatenate([former, latter], axis=0)

    def by_core(rows, which):
        size = features // groups_count
        return jnp.concatenate(
            [
                jnp.where(which == 1, rows[:, at + size : at + 2 * size], rows[:, at : at + size])
                for at in range(0, features, 2 * size)
            ],
            axis=1,
        )

    in_a = ring.gather(block_input[0])
    slice_rows = w_out.shape[0] // groups_count
    gain_rows = jnp.concatenate([attn_gain, mlp_gain, jnp.zeros((16 * features - 2 * width,), bf16)])
    shares = ring.gather(
        jnp.concatenate(
            [
                lax.dynamic_slice_in_dim(w_out, lax.axis_index(DP) * slice_rows, slice_rows, axis=0),
                gain_rows.reshape(16, features),
            ],
            axis=0,
        )
    )
    every.blocks = block_input
    in_a.hop()
    shares.hop()
    pad = jnp.zeros((features, CH - 2 * heads), bf16)
    last = lax.optimization_barrier(jnp.concatenate([w_alpha, w_beta, pad], axis=1))
    every.w_in = jnp.concatenate([w_query, w_key, w_value, w_gate, last], axis=1)
    ring.tick(in_a, shares)
    in_b = ring.gather(every.blocks[1])
    del every.blocks
    in_a.hop()
    shares.hop()
    ring.tick(in_a, shares)
    in_a.hop()
    shares.hop()
    ring.tick(in_a, shares)
    in_b.hop()
    gain_blocks = [block[slice_rows:] for block in shares.blocks()]
    gain_blocks = [block.reshape(-1)[: 2 * width] for block in gain_blocks]
    every.gains = jnp.stack(
        [
            jnp.concatenate([g[:width] for g in gain_blocks]),
            jnp.concatenate([g[width:] for g in gain_blocks]),
        ]
    ).astype(f32)
    normalise(a, in_a.take())
    project(a)
    ring.tick(in_b)
    in_b.hop()
    w_out_full = lax.all_gather(
        jnp.stack([block[:slice_rows] for block in shares.take_blocks()]), DP, axis=1, tiled=True
    ).reshape(-1, features)
    mix(a)
    every.w_ups = [w_mlp_gate, w_mlp_up]
    ring.tick(in_b)
    in_b.hop()
    mixed_a = ring.gather(a.mixed)
    mixed_a.hop()
    every.w_up2 = jnp.concatenate(every.w_ups, axis=1)
    del every.w_ups
    ring.tick(in_b)
    normalise(b, in_b.take())
    project(b)
    ring.tick(mixed_a)
    mixed_a.hop()
    mix(b)
    ring.tick(mixed_a)
    mixed_a.hop()
    mixed_b = ring.gather(b.mixed)
    mixed_b.hop()
    every.w_out = w_out_full
    ring.tick(mixed_a)
    attend(a, mixed_a.take())
    ring.tick(mixed_b)
    mixed_b.hop()
    normalise_mid(a)
    expand(a)
    ring.tick(mixed_b)
    mixed_b.hop()
    activate(a)
    ring.tick(mixed_b)
    back_mid(a)
    ring.tick()
    mid_a = ring.scatter(a.part_mid)
    del a.part_mid
    mid_a.hop()
    attend(b, mixed_b.take())
    ring.tick(mid_a)
    del every.w_out
    mid_a.hop()
    normalise_mid(b)
    expand(b)
    ring.tick(mid_a)
    mid_a.hop()
    activate(b)
    ring.tick(mid_a)
    a.grad_mid_own = mid_a.take()
    back_a = ring.gather(a.grad_mid_own.astype(bf16))
    back_a.hop()
    back_mid(b)
    ring.tick()
    mid_b = ring.scatter(b.part_mid)
    del b.part_mid
    mid_b.hop()
    every.down = matmul_rows(
        rows_of(a.product, b.product), rows_of(grad_output(a), grad_output(b)), bf16
    )
    ring.tick(back_a)
    down_sum = lax.psum_scatter(every.down, DP, scatter_dimension=1, tiled=True)
    del every.down
    back_a.hop()
    every.up2 = matmul_rows(
        rows_of(a.normed_mid, b.normed_mid), rows_of(a.grad_acts, b.grad_acts), bf16
    )
    ring.tick(mid_b)
    del a.normed_mid, b.normed_mid, a.grad_acts, b.grad_acts
    mid_b.hop()
    contract(a)
    contract(b)
    ring.tick(back_a)
    del a.product, b.product
    back_a.hop()
    normed = rows_of(a.normed, b.normed)
    every.normed_away = by_core(normed, 1 - core)
    every.normed_here = by_core(normed, core)
    ring.tick(mid_b)
    del a.normed, b.normed
    mid_b.hop()
    ring.tick(back_a)
    back_hidden(a, back_a.take())
    ring.tick(mid_b)
    b.grad_mid_own = mid_b.take()
    back_b = ring.gather(b.grad_mid_own.astype(bf16))
    back_b.hop()
    mix_back(a, 0)
    every.down_sum = down_sum
    ring.tick(back_b)
    up2_sum = lax.psum_scatter(every.up2, DP, scatter_dimension=0, tiled=True)
    del every.up2
    back_b.hop()
    for sequence in range(1, per_micro):
        mix_back(a, sequence)
    ring.tick(back_b)
    back_b.hop()
    back_in(a)
    ring.tick(back_b)
    out_a = ring.scatter(a.part_out)
    del a.part_out
    out_a.hop()
    back_hidden(b, back_b.take())
    ring.tick()
    in_grad_a = ring.scatter(a.part_in)
    in_grad_a.hop()
    mix_back(b, 0)
    ring.tick(out_a)
    out_a.hop()
    for sequence in range(1, per_micro):
        mix_back(b, sequence)
    ring.tick(in_grad_a)
    in_grad_a.hop()
    every.away = row_major(matmul_rows(every.normed_away, every.grad_pre, bf16))
    ring.tick(out_a)
    del every.normed_away
    out_a.hop()
    got = lax.ppermute(every.away, DP, [(d, d ^ 1) for d in range(groups_count)])
    del every.away
    back_in(b)
    every.up2_sum = up2_sum
    ring.tick(in_grad_a)
    in_grad_a.hop()
    every.total = row_major(
        (matmul_rows(every.normed_here, every.grad_pre) + got.astype(f32)).astype(bf16)
    )
    ring.tick(out_a)
    del every.normed_here, every.grad_pre
    cube = Cube(every.total, 2 * inner, groups_count, ring)
    del every.total
    cube.hop()
    out_b = ring.scatter(b.part_out)
    del b.part_out
    out_b.hop()
    every.out = matmul_rows(rows_of(a.mixed, b.mixed), rows_of(a.grad_low, b.grad_low), bf16)
    gain_in(a)
    gain_in(b)
    ring.tick(in_grad_a)
    del a.mixed, b.mixed, a.grad_low, b.grad_low
    out_sum = lax.psum_scatter(every.out, DP, scatter_dimension=1, tiled=True)
    del every.out
    in_grad_b = ring.scatter(b.part_in)
    in_grad_b.hop()
    del a.part_in, b.part_in
    taps = 3 * TAPS
    sums = Sums(
        ring,
        jnp.concatenate(
            [
                a.dot_in, b.dot_in, a.gain_in + b.gain_in,
                jnp.sum(every.wide[taps].reshape(heads, CH), 0),
            ]
        ),
    )
    sums.around(heads_count)
    every.mlp_gain = jnp.sum(a.grad_mid_own * own_of(a.hidden) * a.scale_mid, 0) + jnp.sum(
        b.grad_mid_own * own_of(b.hidden) * b.scale_mid, 0
    )
    ring.tick(out_b)
    out_b.hop()
    every.down_grad = every.down_sum.astype(f32)
    every.up2_grad = [
        every.up2_sum[:, :hidden_units].astype(f32), every.up2_sum[:, hidden_units:].astype(f32)
    ]
    del every.down_sum, every.up2_sum
    finish_output(a, out_a.take())
    ring.tick(in_grad_b, sums, cube)
    in_grad_b.hop()
    cube.add()
    while cube.todo[0]:
        cube.hop()
        if len(cube.todo[0]) == 1:
            break
        cube.land()
        cube.add()
    [around] = sums.state
    small = Sums(
        ring,
        jnp.concatenate(
            [
                every.wide[:taps].reshape(-1),
                own_of(around[2 * row_count : 2 * row_count + features]),
                every.mlp_gain,
                jnp.pad(around[2 * row_count + features :], (0, inner - CH)),
                jnp.pad(every.decays.reshape(-1), (0, inner - 2 * heads)),
            ]
        ).reshape(-1, CH),
    )
    small.double(groups_count, 1)
    ring.tick(out_b, small)
    out_b.hop()
    finish_input(a, in_grad_a.take(), around[:row_count])
    ring.tick(in_grad_b, cube)
    in_grad_b.hop()
    small.double(groups_count, groups_count)
    cube.add()
    every.out_sum = out_sum
    ring.tick(out_b, small)
    out_grad = every.out_sum.astype(f32)
    finish_output(b, out_b.take())
    every.outputs = jnp.stack([m.output for m in micros])
    ring.tick(in_grad_b)
    finish_input(b, in_grad_b.take(), around[row_count : 2 * row_count])
    in_query_key, in_others = cube.halves
    small = small.state[0].reshape(-1)
    at = taps * inner
    return (
        every.outputs,
        jnp.stack([m.input_grad for m in micros]),
        small[at : at + width],
        in_query_key[:, :inner],
        in_query_key[:, inner:],
        in_others[:, :inner],
        in_others[:, inner : 2 * inner],
        in_others[:, 2 * inner : 2 * inner + heads],
        in_others[:, 2 * inner + heads : 2 * inner + 2 * heads],
        small[:at].reshape(3, TAPS, inner),
        small[at + 2 * width + inner : at + 2 * width + inner + heads],
        small[at + 2 * width + inner + heads : at + 2 * width + inner + 2 * heads],
        small[at + 2 * width : at + 2 * width + CH],
        out_grad,
        small[at + width : at + 2 * width],
        *every.up2_grad,
        every.down_grad,
    )


def solution(mesh):
    each = P(None, HEAD)
    return jax.shard_map(
        functools.partial(body, heads_count=mesh.shape[HEAD], groups_count=mesh.shape[DP]),
        mesh=mesh,
        in_specs=(
            P(None, DP, HEAD), P(None, DP, None), P(None, DP), P(HEAD),
            each, each, each, each, each, each, P(None, None, HEAD), P(HEAD), P(HEAD),
            P(), P(HEAD, None), P(HEAD), each, each, P(HEAD, None),
        ),
        out_specs=(
            P(None, DP, HEAD), P(None, DP, HEAD), P(HEAD),
            P(DP, HEAD), P(DP, HEAD), P(DP, HEAD), P(DP, HEAD),
            P(DP, HEAD), P(DP, HEAD), P(None, None, HEAD), P(HEAD), P(HEAD),
            P(), P(HEAD, DP), P(HEAD), P(DP, HEAD), P(DP, HEAD), P(HEAD, DP),
        ),
        check_vma=False,
    )
```

```python
import functools
import jax
import jax.numpy as jnp
from jax import lax
from jax.experimental import pallas as pl
from jax.experimental.pallas import tpu as pltpu
from jax.experimental.layout import Layout, with_layout_constraint
from jax.sharding import PartitionSpec as P

SEQ = 256
CH = 128
TAPS = 4
epsilon = 1e-06
f32 = jnp.float32
bf16 = jnp.bfloat16


def halves(x):
    high = x.astype(bf16)
    return high, (x - high.astype(f32)).astype(bf16)


def left(x):
    return jnp.concatenate(halves(x), axis=1)


def right(x):
    row = jnp.concatenate(halves(x), axis=1)
    return jnp.concatenate([row, row], axis=0)


def right_t(x):
    high, low = halves(x)
    return jnp.concatenate(
        [jnp.concatenate([high, high], axis=1), jnp.concatenate([low, low], axis=1)], axis=0
    )


def fold(r):
    return r[:, :CH] + r[:, CH:]


def mm(l, r):
    return fold(jnp.dot(l, r, preferred_element_type=f32))


def mm_t(l, r):
    return fold(lax.dot_general(l, r, (((1,), (1,)), ((), ())), preferred_element_type=f32))


def grids():
    row = lax.broadcasted_iota(jnp.int32, (CH, CH), 0)
    col = lax.broadcasted_iota(jnp.int32, (CH, CH), 1)
    return row, col


def sum_matrix(row, col):
    lower = (row >= col).astype(bf16)
    zero = jnp.zeros((CH, CH), bf16)
    return jnp.concatenate(
        [
            jnp.concatenate([lower, jnp.full((CH, CH), -1, bf16)], axis=1),
            jnp.concatenate([lower, zero], axis=1),
            jnp.concatenate([(row < col).astype(bf16), zero], axis=1),
        ],
        axis=0,
    )


def decay_sums(decay, row, col, sums):
    wide = jnp.broadcast_to(decay, (CH, CH))
    cut = jnp.where(row <= col, wide, 0.0)
    r = jnp.concatenate(
        [jnp.concatenate(halves(wide), axis=1), jnp.concatenate(halves(cut), axis=1)], axis=0
    )
    out = fold(jnp.dot(sums, r, preferred_element_type=f32))
    return out[:CH], out[CH : 2 * CH], out[2 * CH :]


def shifted(x, by, row):
    if by == 0:
        return x
    return jnp.where(row >= by, pltpu.roll(x, by, 0), 0.0)


def shifted_back(x, by, row):
    if by == 0:
        return x
    return jnp.where(row < SEQ - by, pltpu.roll(x, SEQ - by, 0), 0.0)


def sigmoid(x):
    return 0.5 + 0.5 * jnp.tanh(0.5 * x)


def conv_sum(x, taps, row):
    total = x * taps[TAPS - 1 : TAPS]
    for by in range(1, TAPS):
        total = total + shifted(x, by, row) * taps[TAPS - 1 - by : TAPS - by]
    return total


def conv_back(x, grad, taps, row):
    grad_x = grad * taps[TAPS - 1 : TAPS]
    sums = [jnp.sum(grad * x, 0, keepdims=True)]
    for by in range(1, TAPS):
        moved = shifted_back(grad, by, row)
        grad_x = grad_x + moved * taps[TAPS - 1 - by : TAPS - by]
        sums.append(jnp.sum(moved * x, 0, keepdims=True))
    return grad_x, jnp.concatenate(sums[::-1], axis=0)


def norm_of(x):
    return lax.rsqrt(jnp.sum(x * x, -1, keepdims=True) + epsilon)


def softplus(x):
    return jnp.maximum(x, 0.0) + jnp.log(1.0 + jnp.exp(-jnp.abs(x)))


def take_turns(workers):
    while workers:
        workers = [worker for worker in workers if next(worker, workers) is None]


def forward_kernel(
    pre_ref, conv_ref, decay_ref, gain_ref,
    mixed_ref, inverse_ref, update_ref, delta_ref,
):
    heads = decay_ref.shape[1]
    inner = heads * CH

    def piece(index, h):
        return slice(index * inner + h * CH, index * inner + (h + 1) * CH)

    row, col = grids()
    long_row = lax.broadcasted_iota(jnp.int32, (SEQ, CH), 0)
    sums = sum_matrix(row, col)
    within = row >= col
    eye = (row == col).astype(f32)
    ab = pre_ref[:, 4 * inner :]
    decay_all = -jnp.exp(decay_ref[0:1, :]) * softplus(ab[:, :heads] + decay_ref[1:2, :])
    strength_all = sigmoid(ab[:, heads : 2 * heads])
    systems, inverses, kept = [None] * 2 * heads, [None] * 2 * heads, [None] * 2 * heads

    def prepare(h):
        at = slice(h * CH, (h + 1) * CH)
        parts = []
        for index in range(3):
            pre = conv_sum(pre_ref[:, piece(index, h)], conv_ref[index][:, at], long_row)
            parts.append(pre * sigmoid(pre))
        queries = parts[0] * norm_of(parts[0]) * CH ** (-0.5)
        keys = parts[1] * norm_of(parts[1])
        yield
        for c in range(2):
            span = slice(c * CH, (c + 1) * CH)
            q, k, v = queries[span], keys[span], parts[2][span]
            spread, start, tail = decay_sums(decay_all[span, h : h + 1], row, col, sums)
            falloff = jnp.where(within, jnp.exp(jnp.minimum(spread, 0.0)), 0.0)
            k_left = left(k)
            both = mm_t(jnp.concatenate([k_left, left(q)], axis=0), right_t(k))
            yield
            beta = jnp.broadcast_to(strength_all[span, h : h + 1], (CH, CH))
            system = jnp.where(row > col, beta * falloff * both[:CH], 0.0)
            systems[2 * h + c] = system
            inverses[2 * h + c] = eye - jnp.where(
                (row // 2 == col // 2) & (row % 2 > col % 2), system, 0.0
            )
            kept[2 * h + c] = (
                q, k_left, v, k, beta, falloff * both[CH:], jnp.exp(start), jnp.exp(tail)
            )

    take_turns([prepare(h) for h in range(heads)])
    size = 2
    while size < CH:
        mask = (row // (2 * size) == col // (2 * size)) & ((row // size) % 2 > (col // size) % 2)
        steps = [
            mm(left(inverse), right(jnp.where(mask, system, 0.0)))
            for inverse, system in zip(inverses, systems)
        ]
        inverses = [
            inverse - mm(left(step), right(inverse)) for inverse, step in zip(inverses, steps)
        ]
        size *= 2

    def solve(h):
        at = slice(h * CH, (h + 1) * CH)
        q, k_left, v, k, beta, scores, start, tail = kept[2 * h]
        first_update = mm(left(inverses[2 * h]), right(beta * v))
        yield
        first_out = mm(left(scores), right(first_update))
        yield
        state = mm(left(k.T), right(tail * first_update))
        yield
        q, k_left, v, k, beta, scores, start, tail = kept[2 * h + 1]
        read = mm(jnp.concatenate([k_left, left(q)], axis=0), right(state))
        yield
        second_update = mm(left(inverses[2 * h + 1]), right(beta * (v - start * read[:CH])))
        yield
        second_out = start * read[CH:] + mm(left(scores), right(second_update))
        yield
        for c, (update, out) in enumerate(((first_update, first_out), (second_update, second_out))):
            span = slice(c * CH, (c + 1) * CH)
            update_ref[span, at] = update
            delta_ref[span, at] = out
            inverse_ref[span, at] = inverses[2 * h + c].T
            scale = lax.rsqrt(jnp.mean(out * out, -1, keepdims=True) + epsilon)
            gate = pre_ref[span, piece(3, h)]
            mixed_ref[span, at] = (
                out * scale * gain_ref[...] * (gate * sigmoid(gate))
            ).astype(bf16)

    take_turns([solve(h) for h in range(heads)])


def backward_kernel(
    pre_ref, conv_ref, decay_ref, gain_ref,
    inverse_ref, update_ref, delta_ref, grad_ref, wide_ref, sums_ref,
    gpre_ref, gwide_ref, gdecay_ref, gdot_ref,
):
    heads = decay_ref.shape[1]
    inner = heads * CH

    def piece(index, h):
        return slice(index * inner + h * CH, index * inner + (h + 1) * CH)

    row, col = grids()
    long_row = lax.broadcasted_iota(jnp.int32, (SEQ, CH), 0)
    sums = sum_matrix(row, col)
    within = row >= col
    strict = row > col
    upper = (row <= col).astype(bf16)
    upper2 = jnp.concatenate([upper, upper], axis=1)
    lower = strict.astype(bf16)
    lower2 = jnp.concatenate([lower, lower], axis=1)
    ab = pre_ref[:, 4 * inner :]
    rate = -jnp.exp(decay_ref[0:1, :])
    shift = ab[:, :heads] + decay_ref[1:2, :]
    decay_all = rate * softplus(shift)
    strength_all = sigmoid(ab[:, heads : 2 * heads])
    grad_decays, grad_strengths, dots = [None] * heads, [None] * heads, [None] * heads

    def one_head(h):
        at = slice(h * CH, (h + 1) * CH)
        pres, parts = [], []
        for index in range(3):
            pre = conv_sum(pre_ref[:, piece(index, h)], conv_ref[index][:, at], long_row)
            pres.append(pre)
            parts.append(pre * sigmoid(pre))
        q_norm, k_norm = norm_of(parts[0]), norm_of(parts[1])
        queries = parts[0] * q_norm * CH ** (-0.5)
        keys = parts[1] * k_norm
        yield
        out = delta_ref[:, at]
        gate = pre_ref[:, piece(3, h)]
        grad = grad_ref[:, at]
        gain = gain_ref[...]
        scale = lax.rsqrt(jnp.mean(out * out, -1, keepdims=True) + epsilon)
        sig = sigmoid(gate)
        scaled = out * scale
        grad_gate = grad * scaled * gain * sig * (1.0 + gate * (1.0 - sig))
        gpre_ref[:, piece(3, h)] = grad_gate.astype(bf16)
        dots[h] = grad_gate * gate
        grad_normed = grad * gate * sig
        norm_gain_sum = jnp.sum(grad_normed * scaled, 0, keepdims=True)
        grad_scaled = grad_normed * gain
        grad_out = scale * (
            grad_scaled - scaled * jnp.mean(grad_scaled * scaled, -1, keepdims=True)
        )
        yield
        stuff = []
        for c in range(2):
            span = slice(c * CH, (c + 1) * CH)
            q, k, v = queries[span], keys[span], parts[2][span]
            spread, start, tail = decay_sums(decay_all[span, h : h + 1], row, col, sums)
            falloff = jnp.where(within, jnp.exp(jnp.minimum(spread, 0.0)), 0.0)
            q_left, k_left = left(q), left(k)
            both = mm_t(jnp.concatenate([k_left, q_left], axis=0), right_t(k))
            yield
            beta = jnp.broadcast_to(strength_all[span, h : h + 1], (CH, CH))
            stuff.append(
                (q, k, v, falloff, both[:CH] * falloff, both[CH:] * falloff, beta,
                 jnp.exp(start), jnp.exp(tail), q_left, k_left)
            )
        carry = None
        grads_q, grads_k, grads_v, grads_g, grads_b = [None] * 2, [None] * 2, [None] * 2, [None] * 2, [None] * 2
        first_update = update_ref[0:CH, at]
        tail_update = stuff[0][8] * first_update
        state = mm(left(stuff[0][1].T), right(tail_update))
        yield
        for c in (1, 0):
            span = slice(c * CH, (c + 1) * CH)
            q, k, v, falloff, similar, scores, beta, start, tail, q_left, k_left = stuff[c]
            update = update_ref[span, at]
            go = grad_out[span]
            grad_update = mm(left(scores.T), right(go))
            yield
            target = v
            if c == 1:
                read = mm(jnp.concatenate([k_left, q_left], axis=0), right(state))
                yield
                target = v - start * read[:CH]
            else:
                pushed = mm(k_left, right(carry))
                yield
                grad_update = grad_update + tail * pushed
            grad_write = mm(left(inverse_ref[span, at]), right(grad_update))
            yield
            outer = mm_t(
                jnp.concatenate([left(grad_write), left(go)], axis=0), right_t(update)
            )
            yield
            grad_system = jnp.where(strict, -outer[:CH], 0.0)
            grad_scores = jnp.where(within, outer[CH:], 0.0)
            grads_b[c] = jnp.sum(grad_write * target + grad_system * similar, -1, keepdims=True)
            grad_target = beta * grad_write
            grads_v[c] = grad_target
            grad_similar = grad_system * beta * falloff
            grad_dots = grad_scores * falloff
            moved = grad_system * beta * similar + grad_scores * scores
            k_right = right(k)
            back = mm(
                jnp.concatenate(
                    [left(grad_dots), left(grad_similar + grad_similar.T)], axis=0
                ),
                k_right,
            )
            yield
            gq = back[:CH]
            gk = back[CH:] + mm(left(grad_dots.T), right(q))
            yield
            if c == 1:
                through_out, through_read = start * go, -start * grad_target
                more = mm_t(
                    jnp.concatenate([left(through_out), left(through_read)], axis=0),
                    right_t(state),
                )
                yield
                gq = gq + more[:CH]
                gk = gk + more[CH:]
                carry = mm(left(q.T), right(through_out)) + mm(left(k.T), right(through_read))
                yield
                other = through_out * read[CH:] + through_read * read[:CH]
                turned = jnp.dot(
                    upper2,
                    jnp.concatenate(
                        [
                            jnp.concatenate([a, b], axis=1)
                            for a, b in zip(halves(moved), halves(other))
                        ],
                        axis=0,
                    ),
                    preferred_element_type=f32,
                )
                turned = jnp.where(strict, turned[:, :CH], 0.0) + turned[:, CH:]
            else:
                gk = gk + mm_t(left(tail_update), right_t(carry))
                yield
                other = pushed * tail_update
                r1 = jnp.dot(upper2, jnp.concatenate(halves(moved), axis=0), preferred_element_type=f32)
                r2 = jnp.dot(lower2, jnp.concatenate(halves(other), axis=0), preferred_element_type=f32)
                turned = jnp.where(strict, r1, 0.0) + r2
            grads_g[c] = jnp.sum(turned, -1, keepdims=True)
            grads_q[c] = gq
            grads_k[c] = gk
        grad_decays[h] = jnp.concatenate(grads_g, axis=0)
        grad_strengths[h] = jnp.concatenate(grads_b, axis=0)
        gq = jnp.concatenate(grads_q, axis=0)
        gk = jnp.concatenate(grads_k, axis=0)
        gv = jnp.concatenate(grads_v, axis=0)
        yield
        unit = parts[0] * q_norm
        gq = (CH ** (-0.5)) * q_norm * (gq - unit * jnp.sum(gq * unit, -1, keepdims=True))
        gk = k_norm * (gk - keys * jnp.sum(gk * keys, -1, keepdims=True))
        for index, g in enumerate((gq, gk, gv)):
            pre = pres[index]
            sig = sigmoid(pre)
            g = g * sig * (1.0 + pre * (1.0 - sig))
            gx, gw = conv_back(pre_ref[:, piece(index, h)], g, conv_ref[index][:, at], long_row)
            gpre_ref[:, piece(index, h)] = gx.astype(bf16)
            dots[h] = dots[h] + gx * pre_ref[:, piece(index, h)]
            taps = slice(TAPS * index, TAPS * (index + 1))
            gwide_ref[taps, at] = wide_ref[taps, at] + gw
        last = slice(3 * TAPS, 3 * TAPS + 1)
        gwide_ref[last, at] = wide_ref[last, at] + norm_gain_sum

    take_turns([one_head(h) for h in range(heads)])
    lane = lax.broadcasted_iota(jnp.int32, (SEQ, CH), 1)
    gd = jnp.zeros((SEQ, CH), f32)
    gs = jnp.zeros((SEQ, CH), f32)
    for h in range(heads):
        gd = jnp.where(lane == h, grad_decays[h], gd)
        gs = jnp.where(lane == heads + h, grad_strengths[h], gs)
    sig = sigmoid(ab)
    grad_shift = gd[:, :heads] * rate * sigmoid(shift)
    gab = gs * sig * (1.0 - sig)
    for h in range(heads):
        gab = jnp.where(lane == h, grad_shift[:, h : h + 1], gab)
    gpre_ref[:, 4 * inner :] = gab.astype(bf16)
    total = jnp.where(lane < 2 * heads, gab * ab, 0.0)
    for h in range(heads):
        total = total + dots[h]
    gdot_ref[...] = jnp.sum(total, -1, keepdims=True)
    gdecay_ref[0:1, :] = sums_ref[0:1, :] + jnp.sum(gd[:, :heads] * decay_all, 0, keepdims=True)
    gdecay_ref[1:2, :] = sums_ref[1:2, :] + jnp.sum(grad_shift, 0, keepdims=True)


def row_spec(width):
    return pl.BlockSpec((SEQ, width), lambda i: (i, 0))


def whole_spec(shape):
    return pl.BlockSpec(shape, lambda i: (0,) * len(shape))


def mixer_forward(pre, conv_weight, decay, gain):
    rows = pre.shape[0]
    heads = decay.shape[1]
    width = heads * CH
    wide = jax.ShapeDtypeStruct((rows, width), f32)
    return pl.pallas_call(
        forward_kernel,
        grid=(rows // SEQ,),
        in_specs=[row_spec(pre.shape[1])]
        + [whole_spec(conv_weight.shape), whole_spec(decay.shape), whole_spec(gain.shape)],
        out_specs=[row_spec(width)] * 4,
        out_shape=[jax.ShapeDtypeStruct((rows, width), bf16), wide, wide, wide],
        compiler_params=pltpu.CompilerParams(vmem_limit_bytes=56 * 2**20),
        cost_estimate=pl.CostEstimate(flops=10**10, bytes_accessed=10**7, transcendentals=0),
        name="mixer_forward",
    )(pre, conv_weight, decay, gain)


def mixer_backward(
    pre, conv_weight, decay, gain, inverse, update, delta, grad, wide, sums, sequence, shared, slot, slots
):
    heads = decay.shape[1]
    width = heads * CH

    def rows(columns):
        return pl.BlockSpec((SEQ, columns), lambda i: (sequence, 0))

    def kernel(*refs):
        backward_kernel(*refs[:10], *refs[-4:])

    operands = [pre, conv_weight, decay, gain, inverse, update, delta, grad, wide, sums]
    in_specs = (
        [rows(pre.shape[1])]
        + [whole_spec(x.shape) for x in (conv_weight, decay, gain)]
        + [rows(width)] * 4
        + [whole_spec(wide.shape), whole_spec(sums.shape)]
    )
    if shared is not None:
        operands.append(shared)
        in_specs.append(pl.BlockSpec(memory_space=pl.ANY))
    return pl.pallas_call(
        kernel,
        grid=(1,),
        in_specs=in_specs,
        out_specs=[
            pl.BlockSpec((SEQ, pre.shape[1]), lambda i: (slot, 0)),
            whole_spec(wide.shape),
            whole_spec(sums.shape),
            pl.BlockSpec((SEQ, 1), lambda i: (0, 0)),
        ],
        out_shape=[
            jax.ShapeDtypeStruct((slots * SEQ, pre.shape[1]), bf16),
            jax.ShapeDtypeStruct(wide.shape, f32),
            jax.ShapeDtypeStruct(sums.shape, f32),
            jax.ShapeDtypeStruct((SEQ, 1), f32),
        ],
        input_output_aliases={} if shared is None else {10: 0},
        compiler_params=pltpu.CompilerParams(vmem_limit_bytes=56 * 2**20),
        cost_estimate=pl.CostEstimate(flops=10**10, bytes_accessed=10**7, transcendentals=0),
        name="mixer_backward",
    )(*operands)


HEAD = "head"
DP = "dp"


def matmul(former, latter, kind=f32):
    return jnp.dot(former, latter, preferred_element_type=f32).astype(kind)


def matmul_rows(former, latter, kind=f32):
    return lax.dot_general(
        former, latter, (((0,), (0,)), ((), ())), preferred_element_type=f32
    ).astype(kind)


def matmul_back(former, latter, kind=f32):
    return lax.dot_general(
        former, latter, (((1,), (1,)), ((), ())), preferred_element_type=f32
    ).astype(kind)


def row_major(x):
    return with_layout_constraint(x, Layout(major_to_minor=tuple(range(x.ndim))))


def ring_order(count):
    return [0] + list(range(1, count, 2)) + [d for d in range(count - 1, 0, -1) if d % 2 == 0]


class Bag:
    pass


class Ring:
    def __init__(self, count):
        self.count = count
        self.order = ring_order(count)
        self.pairs = [(self.order[i], self.order[(i + 1) % count]) for i in range(count)]
        self.me = lax.axis_index(HEAD)
        self.place = self.lookup([self.order.index(d) for d in range(count)], self.me)
        self.bags = []
        self.transfers = []

    def lookup(self, table, index):
        found = jnp.int32(table[0])
        for i in range(1, self.count):
            found = jnp.where(index == i, table[i], found)
        return found

    def bag(self):
        self.bags.append(Bag())
        return self.bags[-1]

    def gather(self, own):
        return Gather(self, own)

    def scatter(self, partial):
        return Scatter(self, partial)

    def tick(self, *landing):
        for transfer in landing:
            transfer.land()
        state = [vars(bag) for bag in self.bags] + [t.state for t in self.transfers]
        flat, tree = jax.tree.flatten(state)
        state = jax.tree.unflatten(tree, lax.optimization_barrier(flat))
        for bag, values in zip(self.bags, state):
            vars(bag).update(values)
        for transfer, values in zip(self.transfers, state[len(self.bags) :]):
            transfer.state = values

    def hops(self, part):
        return [s for s in range(1, self.count) if (s - 1) * 3 // (self.count - 1) == part]

    def send(self, block):
        return lax.ppermute(block, HEAD, self.pairs)


class Gather:
    def __init__(self, ring, own):
        self.ring = ring
        self.state = [own]
        self.air = []
        self.part = 0
        ring.transfers.append(self)

    def hop(self):
        for _ in self.ring.hops(self.part):
            self.air.append(self.ring.send((self.state + self.air)[-1]))
        self.part += 1

    def land(self):
        self.state = self.state + self.air
        self.air = []

    def take(self):
        return jnp.concatenate(self.take_blocks(), axis=1)

    def take_blocks(self):
        self.ring.transfers.remove(self)
        return self.blocks()

    def blocks(self):
        ring = self.ring
        blocks = []
        for block in range(ring.count):
            chosen = self.state[0]
            at = ring.order.index(block)
            for device in range(ring.count):
                back = (ring.order.index(device) - at) % ring.count
                if back:
                    chosen = jnp.where(ring.me == device, self.state[back], chosen)
            blocks.append(chosen)
        return blocks


class Scatter:
    def __init__(self, ring, partial):
        self.ring = ring
        self.state = [partial]
        self.part = 0
        ring.transfers.append(self)

    def block(self, back):
        ring, partial = self.ring, self.state[0]
        width = partial.shape[1] // ring.count
        index = ring.lookup(ring.order, (ring.place + ring.count - back) % ring.count)
        return lax.dynamic_slice_in_dim(partial, index * width, width, axis=1)

    def hop(self):
        for step in self.ring.hops(self.part):
            send = self.block(step)
            if step > 1:
                send = (send.astype(f32) + self.state[1].astype(f32)).astype(bf16)
            self.state = [self.state[0], self.ring.send(send)]
        self.air = self.state.pop()
        self.part += 1

    def land(self):
        self.state = [self.state[0], self.air]

    def take(self):
        self.ring.transfers.remove(self)
        return self.block(0).astype(f32) + self.state[1].astype(f32)


class Cube:
    def __init__(self, total, cut, count, ring):
        self.count = count
        self.me = lax.axis_index(DP)
        bits = list(range(1, count.bit_length() - 1))
        self.halves = [total[:, :cut], total[:, cut:]]
        self.state = []
        self.todo = [bits, bits[::-1]]
        self.left = [list(bits), list(bits)]
        ring.transfers.append(self)

    def pick(self, x, todo, left, flip):
        blocks = 2 ** len(left)
        size = x.shape[0] // blocks
        at = 1 << left.index(todo[0])
        high = (((self.me >> todo[0]) & 1) ^ flip) == 1
        rows = [
            jnp.where(high, x[(i + at) * size : (i + at + 1) * size], x[i * size : (i + 1) * size])
            for i in range(blocks)
            if not i & at
        ]
        return jnp.concatenate(rows, axis=0)

    def hop(self):
        self.air = [
            lax.ppermute(
                self.pick(x, todo, left, 1), DP, [(d, d ^ (1 << todo[0])) for d in range(self.count)]
            )
            for x, todo, left in zip(self.halves, self.todo, self.left)
        ]

    def land(self):
        self.state = self.air

    def add(self):
        halves = []
        for i in range(2):
            x, todo, left, got = self.halves[i], self.todo[i], self.left[i], self.state[i]
            total = self.pick(x, todo, left, 0).astype(f32) + got.astype(f32)
            self.left[i] = [bit for bit in left if bit != todo[0]]
            self.todo[i] = todo[1:]
            halves.append(total.astype(bf16) if self.todo[i] else total)
        self.halves, self.state = halves, []


class Sums:
    def __init__(self, ring, own):
        self.state = [own]
        self.step = 1
        ring.transfers.append(self)

    def around(self, count):
        own = self.state[0]
        self.air = [
            lax.ppermute(own, HEAD, [(d, (d + step) % count) for d in range(count)])
            for step in range(1, count)
        ]

    def double(self, count, times):
        total = self.state[0]
        for _ in range(times):
            if self.step < count:
                total = total + lax.ppermute(total, DP, [(d, d ^ self.step) for d in range(count)])
                self.step *= 2
        self.state, self.air = [], [total]

    def land(self):
        self.state = [sum(self.state + self.air)]


def body(
    block_input, cotangent, seq_count, attn_gain, w_query, w_key, w_value, w_gate,
    w_alpha, w_beta, conv_weight, decay_base, decay_bias, norm_gain, w_out, mlp_gain,
    w_mlp_gate, w_mlp_up, w_down, *, heads_count, groups_count,
):
    micro_count, row_count, width = block_input.shape
    ring = Ring(heads_count)
    every, a, b = ring.bag(), ring.bag(), ring.bag()
    micros = (a, b)
    index = {a: 0, b: 1}
    features = heads_count * width
    heads = decay_base.shape[0]
    hidden_units = w_down.shape[0]
    inner = w_query.shape[1]
    per_micro = row_count // SEQ
    decay = jnp.stack([decay_base, decay_bias])
    gain_row = norm_gain[None]
    attn_own = attn_gain.astype(f32)
    mlp_own = mlp_gain.astype(f32)
    core = lax.axis_index(DP) & 1

    def own_of(values):
        return lax.dynamic_slice_in_dim(values, ring.me * width, width, axis=values.ndim - 1)

    def live_rows(m):
        return (jnp.arange(row_count) // SEQ < seq_count[index[m], 0])[:, None]

    def inputs_own(m):
        return jnp.where(live_rows(m), block_input[index[m]], jnp.zeros((), bf16)).astype(f32)

    def grad_output(m):
        return jnp.where(live_rows(m), cotangent[index[m]], jnp.zeros((), bf16))

    def normalise(m, raw):
        m.low = jnp.where(live_rows(m), raw, jnp.zeros((), bf16))
        inputs = m.low.astype(f32)
        m.scale_in = lax.rsqrt(jnp.mean(inputs * inputs, -1, keepdims=True) + epsilon)
        m.normed = (inputs * m.scale_in * every.gains[:1]).astype(bf16)

    def project(m):
        m.pre = matmul(m.normed, every.w_in)

    def mix(m):
        m.mixed, *m.saved = mixer_forward(m.pre, conv_weight, decay, gain_row)

    def attend(m, mixed):
        m.hidden = m.low.astype(f32) + matmul(mixed, every.w_out)

    def normalise_mid(m):
        hidden = m.hidden
        m.scale_mid = lax.rsqrt(jnp.mean(hidden * hidden, -1, keepdims=True) + epsilon)
        m.normed_mid = (hidden * m.scale_mid * every.gains[1:]).astype(bf16)

    def expand(m):
        m.acts = matmul(m.normed_mid, every.w_up2)

    def activate(m):
        gate_act, up_act = m.acts[:, :hidden_units], m.acts[:, hidden_units:]
        del m.acts
        sig = jax.nn.sigmoid(gate_act)
        silu = gate_act * sig
        m.product = (silu * up_act).astype(bf16)
        grad_product = m.grad_product.astype(f32)
        del m.grad_product
        grad_gate = (grad_product * up_act * sig * (1.0 + gate_act * (1.0 - sig))).astype(bf16)
        grad_up = (grad_product * silu).astype(bf16)
        m.grad_acts = jnp.concatenate([grad_gate, grad_up], axis=1)

    def back_mid(m):
        m.part_mid = matmul_back(m.grad_acts, every.w_up2, bf16)

    def contract(m):
        m.part_out = matmul(m.product, w_down, bf16)

    def back_hidden(m, grad_mid):
        grad_mid = grad_mid.astype(f32)
        scale, gain = m.scale_mid, every.gains[1:]
        dot_mid = jnp.sum(grad_mid * gain * m.hidden, -1, keepdims=True)
        back = scale**3 * dot_mid / features
        out = grad_output(m)
        m.grad_low = (out.astype(f32) + scale * gain * grad_mid - m.hidden * back).astype(bf16)
        m.grad_hidden_own = (
            own_of(out).astype(f32) + scale * mlp_own * m.grad_mid_own - own_of(m.hidden) * back
        )
        m.grad_mixed = matmul_back(m.grad_low, w_out)

    def mix_back(m, sequence):
        slot = index[m] * per_micro + sequence
        every.grad_pre, every.wide, every.decays, dots = mixer_backward(
            m.pre, conv_weight, decay, gain_row, *m.saved, m.grad_mixed,
            every.wide if slot else jnp.zeros((16, inner), f32),
            every.decays if slot else jnp.zeros((2, heads), f32),
            sequence, every.grad_pre if slot else None, slot, micro_count * per_micro,
        )
        m.dots = (m.dots if sequence else []) + [dots]

    def back_in(m):
        grad_pre = every.grad_pre[index[m] * row_count : (index[m] + 1) * row_count]
        m.part_in = matmul_back(grad_pre, every.w_in, bf16)

    def gain_in(m):
        m.gain_in = jnp.sum(m.part_in.astype(f32) * m.low.astype(f32) * m.scale_in, 0)

    def finish_output(m, summed):
        m.output = (own_of(m.hidden) + summed).astype(bf16)

    def finish_input(m, grad_in, dot_in):
        m.input_grad = (
            m.grad_hidden_own
            + m.scale_in * attn_own * grad_in
            - inputs_own(m) * m.scale_in**3 * dot_in[:, None] / features
        )

    def rows_of(former, latter):
        return jnp.concatenate([former, latter], axis=0)

    def by_core(rows, which):
        size = features // groups_count
        return jnp.concatenate(
            [
                jnp.where(which == 1, rows[:, at + size : at + 2 * size], rows[:, at : at + size])
                for at in range(0, features, 2 * size)
            ],
            axis=1,
        )

    in_a = ring.gather(block_input[0])
    slice_rows = w_out.shape[0] // groups_count
    gain_rows = jnp.pad(jnp.stack([attn_gain, mlp_gain]), ((0, 14), (0, features - width)))
    shares = ring.gather(
        jnp.concatenate(
            [
                lax.dynamic_slice_in_dim(w_out, lax.axis_index(DP) * slice_rows, slice_rows, axis=0),
                gain_rows,
            ],
            axis=0,
        )
    )
    every.blocks = block_input
    in_a.hop()
    shares.hop()
    pad = jnp.zeros((features, CH - 2 * heads), bf16)
    last = lax.optimization_barrier(jnp.concatenate([w_alpha, w_beta, pad], axis=1))
    every.w_in = jnp.concatenate([w_query, w_key, w_value, w_gate, last], axis=1)
    ring.tick(in_a, shares)
    in_b = ring.gather(every.blocks[1])
    del every.blocks
    in_a.hop()
    shares.hop()
    for m in micros:
        m.grad_product = matmul_back(grad_output(m), w_down, bf16)
    ring.tick(in_a, shares)
    in_a.hop()
    shares.hop()
    ring.tick(in_a, shares)
    in_b.hop()
    every.gains = jnp.concatenate(
        [block[slice_rows : slice_rows + 2, :width] for block in shares.blocks()], axis=1
    ).astype(f32)
    normalise(a, in_a.take())
    project(a)
    ring.tick(in_b)
    in_b.hop()
    w_out_full = lax.all_gather(
        jnp.stack([block[:slice_rows] for block in shares.take_blocks()]), DP, axis=1, tiled=True
    ).reshape(-1, features)
    mix(a)
    every.w_ups = [w_mlp_gate, w_mlp_up]
    ring.tick(in_b)
    in_b.hop()
    mixed_a = ring.gather(a.mixed)
    mixed_a.hop()
    every.w_up2 = jnp.concatenate(every.w_ups, axis=1)
    del every.w_ups
    ring.tick(in_b)
    normalise(b, in_b.take())
    project(b)
    ring.tick(mixed_a)
    mixed_a.hop()
    mix(b)
    ring.tick(mixed_a)
    mixed_a.hop()
    mixed_b = ring.gather(b.mixed)
    mixed_b.hop()
    every.w_out = w_out_full
    ring.tick(mixed_a)
    attend(a, mixed_a.take())
    ring.tick(mixed_b)
    mixed_b.hop()
    normalise_mid(a)
    expand(a)
    ring.tick(mixed_b)
    mixed_b.hop()
    activate(a)
    back_mid(a)
    ring.tick(mixed_b)
    mid_a = ring.scatter(a.part_mid)
    del a.part_mid
    mid_a.hop()
    attend(b, mixed_b.take())
    ring.tick(mid_a)
    del every.w_out
    mid_a.hop()
    normalise_mid(b)
    expand(b)
    ring.tick(mid_a)
    mid_a.hop()
    activate(b)
    ring.tick(mid_a)
    a.grad_mid_own = mid_a.take()
    back_a = ring.gather(a.grad_mid_own.astype(bf16))
    back_a.hop()
    back_mid(b)
    ring.tick()
    mid_b = ring.scatter(b.part_mid)
    del b.part_mid
    mid_b.hop()
    every.down = matmul_rows(
        rows_of(a.product, b.product), rows_of(grad_output(a), grad_output(b)), bf16
    )
    ring.tick(back_a)
    down_sum = lax.psum_scatter(every.down, DP, scatter_dimension=1, tiled=True)
    del every.down
    back_a.hop()
    every.up2 = matmul_rows(
        rows_of(a.normed_mid, b.normed_mid), rows_of(a.grad_acts, b.grad_acts), bf16
    )
    ring.tick(mid_b)
    del a.normed_mid, b.normed_mid, a.grad_acts, b.grad_acts
    mid_b.hop()
    contract(a)
    contract(b)
    ring.tick(back_a)
    del a.product, b.product
    back_a.hop()
    normed = rows_of(a.normed, b.normed)
    every.normed_away = by_core(normed, 1 - core)
    every.normed_here = by_core(normed, core)
    ring.tick(mid_b)
    del a.normed, b.normed
    mid_b.hop()
    ring.tick(back_a)
    back_hidden(a, back_a.take())
    ring.tick(mid_b)
    b.grad_mid_own = mid_b.take()
    back_b = ring.gather(b.grad_mid_own.astype(bf16))
    back_b.hop()
    mix_back(a, 0)
    every.down_sum = down_sum
    ring.tick(back_b)
    up2_sum = lax.psum_scatter(every.up2, DP, scatter_dimension=0, tiled=True)
    del every.up2
    back_b.hop()
    for sequence in range(1, per_micro):
        mix_back(a, sequence)
    ring.tick(back_b)
    back_b.hop()
    back_in(a)
    ring.tick(back_b)
    out_a = ring.scatter(a.part_out)
    del a.part_out
    out_a.hop()
    back_hidden(b, back_b.take())
    ring.tick()
    in_grad_a = ring.scatter(a.part_in)
    in_grad_a.hop()
    mix_back(b, 0)
    ring.tick(out_a)
    out_a.hop()
    for sequence in range(1, per_micro):
        mix_back(b, sequence)
    ring.tick(in_grad_a)
    in_grad_a.hop()
    every.away = row_major(matmul_rows(every.normed_away, every.grad_pre, bf16))
    ring.tick(out_a)
    del every.normed_away
    out_a.hop()
    got = lax.ppermute(every.away, DP, [(d, d ^ 1) for d in range(groups_count)])
    del every.away
    back_in(b)
    every.up2_sum = up2_sum
    ring.tick(in_grad_a)
    in_grad_a.hop()
    every.total = row_major(
        (matmul_rows(every.normed_here, every.grad_pre) + got.astype(f32)).astype(bf16)
    )
    ring.tick(out_a)
    del every.normed_here, every.grad_pre
    cube = Cube(every.total, 2 * inner, groups_count, ring)
    del every.total
    cube.hop()
    out_b = ring.scatter(b.part_out)
    del b.part_out
    out_b.hop()
    every.out = matmul_rows(rows_of(a.mixed, b.mixed), rows_of(a.grad_low, b.grad_low), bf16)
    gain_in(a)
    gain_in(b)
    ring.tick(in_grad_a)
    del a.mixed, b.mixed, a.grad_low, b.grad_low
    out_sum = lax.psum_scatter(every.out, DP, scatter_dimension=1, tiled=True)
    del every.out
    in_grad_b = ring.scatter(b.part_in)
    in_grad_b.hop()
    del a.part_in, b.part_in
    taps = 3 * TAPS
    dots = jnp.concatenate(
        [jnp.concatenate(m.dots, axis=0) / m.scale_in for m in micros], axis=0
    ).reshape(-1)
    sums = Sums(
        ring,
        jnp.concatenate(
            [
                dots, a.gain_in + b.gain_in,
                jnp.sum(every.wide[taps].reshape(heads, CH), 0),
            ]
        ),
    )
    sums.around(heads_count)
    every.mlp_gain = jnp.sum(a.grad_mid_own * own_of(a.hidden) * a.scale_mid, 0) + jnp.sum(
        b.grad_mid_own * own_of(b.hidden) * b.scale_mid, 0
    )
    ring.tick(out_b)
    out_b.hop()
    every.down_grad = every.down_sum.astype(f32)
    every.up2_grad = [
        every.up2_sum[:, :hidden_units].astype(f32), every.up2_sum[:, hidden_units:].astype(f32)
    ]
    del every.down_sum, every.up2_sum
    finish_output(a, out_a.take())
    ring.tick(in_grad_b, sums, cube)
    in_grad_b.hop()
    cube.add()
    while cube.todo[0]:
        cube.hop()
        if len(cube.todo[0]) == 1:
            break
        cube.land()
        cube.add()
    [around] = sums.state
    small = Sums(
        ring,
        jnp.concatenate(
            [
                every.wide[:taps].reshape(-1),
                own_of(around[2 * row_count : 2 * row_count + features]),
                every.mlp_gain,
                jnp.pad(around[2 * row_count + features :], (0, inner - CH)),
                jnp.pad(every.decays.reshape(-1), (0, inner - 2 * heads)),
            ]
        ).reshape(-1, CH),
    )
    small.double(groups_count, 1)
    ring.tick(out_b, small)
    out_b.hop()
    finish_input(a, in_grad_a.take(), around[:row_count])
    ring.tick(in_grad_b, cube)
    in_grad_b.hop()
    small.double(groups_count, groups_count)
    cube.add()
    every.out_sum = out_sum
    ring.tick(out_b, small)
    out_grad = every.out_sum.astype(f32)
    finish_output(b, out_b.take())
    every.outputs = jnp.stack([m.output for m in micros])
    ring.tick(in_grad_b)
    finish_input(b, in_grad_b.take(), around[row_count : 2 * row_count])
    in_query_key, in_others = cube.halves
    small = small.state[0].reshape(-1)
    at = taps * inner
    return (
        every.outputs,
        jnp.stack([m.input_grad for m in micros]),
        small[at : at + width],
        in_query_key[:, :inner],
        in_query_key[:, inner:],
        in_others[:, :inner],
        in_others[:, inner : 2 * inner],
        in_others[:, 2 * inner : 2 * inner + heads],
        in_others[:, 2 * inner + heads : 2 * inner + 2 * heads],
        small[:at].reshape(3, TAPS, inner),
        small[at + 2 * width + inner : at + 2 * width + inner + heads],
        small[at + 2 * width + inner + heads : at + 2 * width + inner + 2 * heads],
        small[at + 2 * width : at + 2 * width + CH],
        out_grad,
        small[at + width : at + 2 * width],
        *every.up2_grad,
        every.down_grad,
    )


def solution(mesh):
    each = P(None, HEAD)
    return jax.shard_map(
        functools.partial(body, heads_count=mesh.shape[HEAD], groups_count=mesh.shape[DP]),
        mesh=mesh,
        in_specs=(
            P(None, DP, HEAD), P(None, DP, None), P(None, DP), P(HEAD),
            each, each, each, each, each, each, P(None, None, HEAD), P(HEAD), P(HEAD),
            P(), P(HEAD, None), P(HEAD), each, each, P(HEAD, None),
        ),
        out_specs=(
            P(None, DP, HEAD), P(None, DP, HEAD), P(HEAD),
            P(DP, HEAD), P(DP, HEAD), P(DP, HEAD), P(DP, HEAD),
            P(DP, HEAD), P(DP, HEAD), P(None, None, HEAD), P(HEAD), P(HEAD),
            P(), P(HEAD, DP), P(HEAD), P(DP, HEAD), P(DP, HEAD), P(HEAD, DP),
        ),
        check_vma=False,
    )
```

```python
import functools
import jax
import jax.numpy as jnp
from jax import lax
from jax.experimental import pallas as pl
from jax.experimental.pallas import tpu as pltpu
from jax.experimental.layout import Layout, with_layout_constraint
from jax.sharding import PartitionSpec as P

SEQ = 256
CH = 128
TAPS = 4
epsilon = 1e-06
f32 = jnp.float32
bf16 = jnp.bfloat16


def halves(x):
    high = x.astype(bf16)
    return high, (x - high.astype(f32)).astype(bf16)


def left(x):
    return jnp.concatenate(halves(x), axis=1)


def right(x):
    row = jnp.concatenate(halves(x), axis=1)
    return jnp.concatenate([row, row], axis=0)


def right_t(x):
    high, low = halves(x)
    return jnp.concatenate(
        [jnp.concatenate([high, high], axis=1), jnp.concatenate([low, low], axis=1)], axis=0
    )


def fold(r):
    return r[:, :CH] + r[:, CH:]


def mm(l, r):
    return fold(jnp.dot(l, r, preferred_element_type=f32))


def mm_t(l, r):
    return fold(lax.dot_general(l, r, (((1,), (1,)), ((), ())), preferred_element_type=f32))


def grids():
    row = lax.broadcasted_iota(jnp.int32, (CH, CH), 0)
    col = lax.broadcasted_iota(jnp.int32, (CH, CH), 1)
    return row, col


def sum_matrix(row, col):
    lower = (row >= col).astype(bf16)
    zero = jnp.zeros((CH, CH), bf16)
    return jnp.concatenate(
        [
            jnp.concatenate([lower, jnp.full((CH, CH), -1, bf16)], axis=1),
            jnp.concatenate([lower, zero], axis=1),
            jnp.concatenate([(row < col).astype(bf16), zero], axis=1),
        ],
        axis=0,
    )


def decay_sums(decay, row, col, sums):
    wide = jnp.broadcast_to(decay, (CH, CH))
    cut = jnp.where(row <= col, wide, 0.0)
    r = jnp.concatenate(
        [jnp.concatenate(halves(wide), axis=1), jnp.concatenate(halves(cut), axis=1)], axis=0
    )
    out = fold(jnp.dot(sums, r, preferred_element_type=f32))
    return out[:CH], out[CH : 2 * CH], out[2 * CH :]


def shifted(x, by, row):
    if by == 0:
        return x
    return jnp.where(row >= by, pltpu.roll(x, by, 0), 0.0)


def shifted_back(x, by, row):
    if by == 0:
        return x
    return jnp.where(row < SEQ - by, pltpu.roll(x, SEQ - by, 0), 0.0)


def sigmoid(x):
    return 0.5 + 0.5 * jnp.tanh(0.5 * x)


def conv_sum(x, taps, row):
    total = x * taps[TAPS - 1 : TAPS]
    for by in range(1, TAPS):
        total = total + shifted(x, by, row) * taps[TAPS - 1 - by : TAPS - by]
    return total


def conv_back(x, grad, taps, row):
    grad_x = grad * taps[TAPS - 1 : TAPS]
    sums = [jnp.sum(grad * x, 0, keepdims=True)]
    for by in range(1, TAPS):
        moved = shifted_back(grad, by, row)
        grad_x = grad_x + moved * taps[TAPS - 1 - by : TAPS - by]
        sums.append(jnp.sum(moved * x, 0, keepdims=True))
    return grad_x, jnp.concatenate(sums[::-1], axis=0)


def norm_of(x):
    return lax.rsqrt(jnp.sum(x * x, -1, keepdims=True) + epsilon)


def softplus(x):
    return jnp.maximum(x, 0.0) + jnp.log(1.0 + jnp.exp(-jnp.abs(x)))


def take_turns(workers):
    while workers:
        workers = [worker for worker in workers if next(worker, workers) is None]


def forward_kernel(
    pre_ref, conv_ref, decay_ref, gain_ref,
    mixed_ref, inverse_ref, update_ref, delta_ref,
):
    heads = decay_ref.shape[1]
    inner = heads * CH

    def piece(index, h):
        return slice(index * inner + h * CH, index * inner + (h + 1) * CH)

    row, col = grids()
    long_row = lax.broadcasted_iota(jnp.int32, (SEQ, CH), 0)
    sums = sum_matrix(row, col)
    within = row >= col
    eye = (row == col).astype(f32)
    ab = pre_ref[:, 4 * inner :]
    decay_all = -jnp.exp(decay_ref[0:1, :]) * softplus(ab[:, :heads] + decay_ref[1:2, :])
    strength_all = sigmoid(ab[:, heads : 2 * heads])
    systems, inverses, kept = [None] * 2 * heads, [None] * 2 * heads, [None] * 2 * heads

    def prepare(h):
        at = slice(h * CH, (h + 1) * CH)
        parts = []
        for index in range(3):
            pre = conv_sum(pre_ref[:, piece(index, h)], conv_ref[index][:, at], long_row)
            parts.append(pre * sigmoid(pre))
        queries = parts[0] * norm_of(parts[0]) * CH ** (-0.5)
        keys = parts[1] * norm_of(parts[1])
        yield
        for c in range(2):
            span = slice(c * CH, (c + 1) * CH)
            q, k, v = queries[span], keys[span], parts[2][span]
            spread, start, tail = decay_sums(decay_all[span, h : h + 1], row, col, sums)
            falloff = jnp.where(within, jnp.exp(jnp.minimum(spread, 0.0)), 0.0)
            k_left = left(k)
            both = mm_t(jnp.concatenate([k_left, left(q)], axis=0), right_t(k))
            yield
            beta = jnp.broadcast_to(strength_all[span, h : h + 1], (CH, CH))
            system = jnp.where(row > col, beta * falloff * both[:CH], 0.0)
            systems[2 * h + c] = system
            inverses[2 * h + c] = eye - jnp.where(
                (row // 2 == col // 2) & (row % 2 > col % 2), system, 0.0
            )
            kept[2 * h + c] = (
                q, k_left, v, k, beta, falloff * both[CH:], jnp.exp(start), jnp.exp(tail)
            )

    take_turns([prepare(h) for h in range(heads)])
    size = 2
    while size < CH:
        mask = (row // (2 * size) == col // (2 * size)) & ((row // size) % 2 > (col // size) % 2)
        steps = [
            mm(left(inverse), right(jnp.where(mask, system, 0.0)))
            for inverse, system in zip(inverses, systems)
        ]
        inverses = [
            inverse - mm(left(step), right(inverse)) for inverse, step in zip(inverses, steps)
        ]
        size *= 2

    def solve(h):
        at = slice(h * CH, (h + 1) * CH)
        q, k_left, v, k, beta, scores, start, tail = kept[2 * h]
        first_update = mm(left(inverses[2 * h]), right(beta * v))
        yield
        first_out = mm(left(scores), right(first_update))
        yield
        state = mm(left(k.T), right(tail * first_update))
        yield
        q, k_left, v, k, beta, scores, start, tail = kept[2 * h + 1]
        read = mm(jnp.concatenate([k_left, left(q)], axis=0), right(state))
        yield
        second_update = mm(left(inverses[2 * h + 1]), right(beta * (v - start * read[:CH])))
        yield
        second_out = start * read[CH:] + mm(left(scores), right(second_update))
        yield
        for c, (update, out) in enumerate(((first_update, first_out), (second_update, second_out))):
            span = slice(c * CH, (c + 1) * CH)
            update_ref[span, at] = update
            delta_ref[span, at] = out
            inverse_ref[span, at] = inverses[2 * h + c].T
            scale = lax.rsqrt(jnp.mean(out * out, -1, keepdims=True) + epsilon)
            gate = pre_ref[span, piece(3, h)]
            mixed_ref[span, at] = (
                out * scale * gain_ref[...] * (gate * sigmoid(gate))
            ).astype(bf16)

    take_turns([solve(h) for h in range(heads)])


def backward_kernel(
    pre_ref, conv_ref, decay_ref, gain_ref,
    inverse_ref, update_ref, delta_ref, grad_ref, wide_ref, sums_ref,
    gpre_ref, gwide_ref, gdecay_ref, gdot_ref,
):
    heads = decay_ref.shape[1]
    inner = heads * CH

    def piece(index, h):
        return slice(index * inner + h * CH, index * inner + (h + 1) * CH)

    row, col = grids()
    long_row = lax.broadcasted_iota(jnp.int32, (SEQ, CH), 0)
    sums = sum_matrix(row, col)
    within = row >= col
    strict = row > col
    upper = (row <= col).astype(bf16)
    upper2 = jnp.concatenate([upper, upper], axis=1)
    lower = strict.astype(bf16)
    lower2 = jnp.concatenate([lower, lower], axis=1)
    ab = pre_ref[:, 4 * inner :]
    rate = -jnp.exp(decay_ref[0:1, :])
    shift = ab[:, :heads] + decay_ref[1:2, :]
    decay_all = rate * softplus(shift)
    strength_all = sigmoid(ab[:, heads : 2 * heads])
    grad_decays, grad_strengths, dots = [None] * heads, [None] * heads, [None] * heads

    def one_head(h):
        at = slice(h * CH, (h + 1) * CH)
        pres, parts = [], []
        for index in range(3):
            pre = conv_sum(pre_ref[:, piece(index, h)], conv_ref[index][:, at], long_row)
            pres.append(pre)
            parts.append(pre * sigmoid(pre))
        q_norm, k_norm = norm_of(parts[0]), norm_of(parts[1])
        queries = parts[0] * q_norm * CH ** (-0.5)
        keys = parts[1] * k_norm
        yield
        out = delta_ref[:, at]
        gate = pre_ref[:, piece(3, h)]
        grad = grad_ref[:, at]
        gain = gain_ref[...]
        scale = lax.rsqrt(jnp.mean(out * out, -1, keepdims=True) + epsilon)
        sig = sigmoid(gate)
        scaled = out * scale
        grad_gate = grad * scaled * gain * sig * (1.0 + gate * (1.0 - sig))
        gpre_ref[:, piece(3, h)] = grad_gate.astype(bf16)
        dots[h] = grad_gate * gate
        grad_normed = grad * gate * sig
        norm_gain_sum = jnp.sum(grad_normed * scaled, 0, keepdims=True)
        grad_scaled = grad_normed * gain
        grad_out = scale * (
            grad_scaled - scaled * jnp.mean(grad_scaled * scaled, -1, keepdims=True)
        )
        yield
        stuff = []
        for c in range(2):
            span = slice(c * CH, (c + 1) * CH)
            q, k, v = queries[span], keys[span], parts[2][span]
            spread, start, tail = decay_sums(decay_all[span, h : h + 1], row, col, sums)
            falloff = jnp.where(within, jnp.exp(jnp.minimum(spread, 0.0)), 0.0)
            q_left, k_left = left(q), left(k)
            both = mm_t(jnp.concatenate([k_left, q_left], axis=0), right_t(k))
            yield
            beta = jnp.broadcast_to(strength_all[span, h : h + 1], (CH, CH))
            stuff.append(
                (q, k, v, falloff, both[:CH] * falloff, both[CH:] * falloff, beta,
                 jnp.exp(start), jnp.exp(tail), q_left, k_left)
            )
        carry = None
        grads_q, grads_k, grads_v, grads_g, grads_b = [None] * 2, [None] * 2, [None] * 2, [None] * 2, [None] * 2
        first_update = update_ref[0:CH, at]
        tail_update = stuff[0][8] * first_update
        state = mm(left(stuff[0][1].T), right(tail_update))
        yield
        for c in (1, 0):
            span = slice(c * CH, (c + 1) * CH)
            q, k, v, falloff, similar, scores, beta, start, tail, q_left, k_left = stuff[c]
            update = update_ref[span, at]
            go = grad_out[span]
            grad_update = mm(left(scores.T), right(go))
            yield
            target = v
            if c == 1:
                read = mm(jnp.concatenate([k_left, q_left], axis=0), right(state))
                yield
                target = v - start * read[:CH]
            else:
                pushed = mm(k_left, right(carry))
                yield
                grad_update = grad_update + tail * pushed
            grad_write = mm(left(inverse_ref[span, at]), right(grad_update))
            yield
            outer = mm_t(
                jnp.concatenate([left(grad_write), left(go)], axis=0), right_t(update)
            )
            yield
            grad_system = jnp.where(strict, -outer[:CH], 0.0)
            grad_scores = jnp.where(within, outer[CH:], 0.0)
            grads_b[c] = jnp.sum(grad_write * target + grad_system * similar, -1, keepdims=True)
            grad_target = beta * grad_write
            grads_v[c] = grad_target
            grad_similar = grad_system * beta * falloff
            grad_dots = grad_scores * falloff
            moved = grad_system * beta * similar + grad_scores * scores
            k_right = right(k)
            back = mm(
                jnp.concatenate(
                    [left(grad_dots), left(grad_similar + grad_similar.T)], axis=0
                ),
                k_right,
            )
            yield
            gq = back[:CH]
            gk = back[CH:] + mm(left(grad_dots.T), right(q))
            yield
            if c == 1:
                through_out, through_read = start * go, -start * grad_target
                more = mm_t(
                    jnp.concatenate([left(through_out), left(through_read)], axis=0),
                    right_t(state),
                )
                yield
                gq = gq + more[:CH]
                gk = gk + more[CH:]
                carry = mm(left(q.T), right(through_out)) + mm(left(k.T), right(through_read))
                yield
                other = through_out * read[CH:] + through_read * read[:CH]
                turned = jnp.dot(
                    upper2,
                    jnp.concatenate(
                        [
                            jnp.concatenate([a, b], axis=1)
                            for a, b in zip(halves(moved), halves(other))
                        ],
                        axis=0,
                    ),
                    preferred_element_type=f32,
                )
                turned = jnp.where(strict, turned[:, :CH], 0.0) + turned[:, CH:]
            else:
                gk = gk + mm_t(left(tail_update), right_t(carry))
                yield
                other = pushed * tail_update
                r1 = jnp.dot(upper2, jnp.concatenate(halves(moved), axis=0), preferred_element_type=f32)
                r2 = jnp.dot(lower2, jnp.concatenate(halves(other), axis=0), preferred_element_type=f32)
                turned = jnp.where(strict, r1, 0.0) + r2
            grads_g[c] = jnp.sum(turned, -1, keepdims=True)
            grads_q[c] = gq
            grads_k[c] = gk
        grad_decays[h] = jnp.concatenate(grads_g, axis=0)
        grad_strengths[h] = jnp.concatenate(grads_b, axis=0)
        gq = jnp.concatenate(grads_q, axis=0)
        gk = jnp.concatenate(grads_k, axis=0)
        gv = jnp.concatenate(grads_v, axis=0)
        yield
        unit = parts[0] * q_norm
        gq = (CH ** (-0.5)) * q_norm * (gq - unit * jnp.sum(gq * unit, -1, keepdims=True))
        gk = k_norm * (gk - keys * jnp.sum(gk * keys, -1, keepdims=True))
        for index, g in enumerate((gq, gk, gv)):
            pre = pres[index]
            sig = sigmoid(pre)
            g = g * sig * (1.0 + pre * (1.0 - sig))
            gx, gw = conv_back(pre_ref[:, piece(index, h)], g, conv_ref[index][:, at], long_row)
            gpre_ref[:, piece(index, h)] = gx.astype(bf16)
            dots[h] = dots[h] + gx * pre_ref[:, piece(index, h)]
            taps = slice(TAPS * index, TAPS * (index + 1))
            gwide_ref[taps, at] = wide_ref[taps, at] + gw
        last = slice(3 * TAPS, 3 * TAPS + 1)
        gwide_ref[last, at] = wide_ref[last, at] + norm_gain_sum

    take_turns([one_head(h) for h in range(heads)])
    lane = lax.broadcasted_iota(jnp.int32, (SEQ, CH), 1)
    gd = jnp.zeros((SEQ, CH), f32)
    gs = jnp.zeros((SEQ, CH), f32)
    for h in range(heads):
        gd = jnp.where(lane == h, grad_decays[h], gd)
        gs = jnp.where(lane == heads + h, grad_strengths[h], gs)
    sig = sigmoid(ab)
    grad_shift = gd[:, :heads] * rate * sigmoid(shift)
    gab = gs * sig * (1.0 - sig)
    for h in range(heads):
        gab = jnp.where(lane == h, grad_shift[:, h : h + 1], gab)
    gpre_ref[:, 4 * inner :] = gab.astype(bf16)
    total = jnp.where(lane < 2 * heads, gab * ab, 0.0)
    for h in range(heads):
        total = total + dots[h]
    gdot_ref[...] = jnp.sum(total, -1, keepdims=True)
    gdecay_ref[0:1, :] = sums_ref[0:1, :] + jnp.sum(gd[:, :heads] * decay_all, 0, keepdims=True)
    gdecay_ref[1:2, :] = sums_ref[1:2, :] + jnp.sum(grad_shift, 0, keepdims=True)


def row_spec(width):
    return pl.BlockSpec((SEQ, width), lambda i: (i, 0))


def whole_spec(shape):
    return pl.BlockSpec(shape, lambda i: (0,) * len(shape))


def mixer_forward(pre, conv_weight, decay, gain):
    rows = pre.shape[0]
    heads = decay.shape[1]
    width = heads * CH
    wide = jax.ShapeDtypeStruct((rows, width), f32)
    return pl.pallas_call(
        forward_kernel,
        grid=(rows // SEQ,),
        in_specs=[row_spec(pre.shape[1])]
        + [whole_spec(conv_weight.shape), whole_spec(decay.shape), whole_spec(gain.shape)],
        out_specs=[row_spec(width)] * 4,
        out_shape=[jax.ShapeDtypeStruct((rows, width), bf16), wide, wide, wide],
        compiler_params=pltpu.CompilerParams(vmem_limit_bytes=56 * 2**20),
        cost_estimate=pl.CostEstimate(flops=10**10, bytes_accessed=10**7, transcendentals=0),
        name="mixer_forward",
    )(pre, conv_weight, decay, gain)


def mixer_backward(
    pre, conv_weight, decay, gain, inverse, update, delta, grad, wide, sums, sequence, shared, slot, slots
):
    heads = decay.shape[1]
    width = heads * CH

    def rows(columns):
        return pl.BlockSpec((SEQ, columns), lambda i: (sequence, 0))

    def kernel(*refs):
        backward_kernel(*refs[:10], *refs[-4:])

    operands = [pre, conv_weight, decay, gain, inverse, update, delta, grad, wide, sums]
    in_specs = (
        [rows(pre.shape[1])]
        + [whole_spec(x.shape) for x in (conv_weight, decay, gain)]
        + [rows(width)] * 4
        + [whole_spec(wide.shape), whole_spec(sums.shape)]
    )
    if shared is not None:
        operands.append(shared)
        in_specs.append(pl.BlockSpec(memory_space=pl.ANY))
    return pl.pallas_call(
        kernel,
        grid=(1,),
        in_specs=in_specs,
        out_specs=[
            pl.BlockSpec((SEQ, pre.shape[1]), lambda i: (slot, 0)),
            whole_spec(wide.shape),
            whole_spec(sums.shape),
            pl.BlockSpec((SEQ, 1), lambda i: (0, 0)),
        ],
        out_shape=[
            jax.ShapeDtypeStruct((slots * SEQ, pre.shape[1]), bf16),
            jax.ShapeDtypeStruct(wide.shape, f32),
            jax.ShapeDtypeStruct(sums.shape, f32),
            jax.ShapeDtypeStruct((SEQ, 1), f32),
        ],
        input_output_aliases={} if shared is None else {10: 0},
        compiler_params=pltpu.CompilerParams(vmem_limit_bytes=56 * 2**20),
        cost_estimate=pl.CostEstimate(flops=10**10, bytes_accessed=10**7, transcendentals=0),
        name="mixer_backward",
    )(*operands)


HEAD = "head"
DP = "dp"


def matmul(former, latter, kind=f32):
    return jnp.dot(former, latter, preferred_element_type=f32).astype(kind)


def matmul_rows(former, latter, kind=f32):
    return lax.dot_general(
        former, latter, (((0,), (0,)), ((), ())), preferred_element_type=f32
    ).astype(kind)


def matmul_back(former, latter, kind=f32):
    return lax.dot_general(
        former, latter, (((1,), (1,)), ((), ())), preferred_element_type=f32
    ).astype(kind)


def row_major(x):
    return with_layout_constraint(x, Layout(major_to_minor=tuple(range(x.ndim))))


def ring_order(count):
    return [0] + list(range(1, count, 2)) + [d for d in range(count - 1, 0, -1) if d % 2 == 0]


class Bag:
    pass


class Ring:
    def __init__(self, count):
        self.count = count
        self.order = ring_order(count)
        self.pairs = [(self.order[i], self.order[(i + 1) % count]) for i in range(count)]
        self.me = lax.axis_index(HEAD)
        self.place = self.lookup([self.order.index(d) for d in range(count)], self.me)
        self.bags = []
        self.transfers = []

    def lookup(self, table, index):
        found = jnp.int32(table[0])
        for i in range(1, self.count):
            found = jnp.where(index == i, table[i], found)
        return found

    def bag(self):
        self.bags.append(Bag())
        return self.bags[-1]

    def gather(self, own):
        return Gather(self, own)

    def scatter(self, partial):
        return Scatter(self, partial)

    def tick(self, *landing):
        for transfer in landing:
            transfer.land()
        state = [vars(bag) for bag in self.bags] + [t.state for t in self.transfers]
        flat, tree = jax.tree.flatten(state)
        state = jax.tree.unflatten(tree, lax.optimization_barrier(flat))
        for bag, values in zip(self.bags, state):
            vars(bag).update(values)
        for transfer, values in zip(self.transfers, state[len(self.bags) :]):
            transfer.state = values

    def hops(self, part):
        return [s for s in range(1, self.count) if (s - 1) * 3 // (self.count - 1) == part]

    def send(self, block):
        return lax.ppermute(block, HEAD, self.pairs)


class Gather:
    def __init__(self, ring, own):
        self.ring = ring
        self.state = [own]
        self.air = []
        self.part = 0
        ring.transfers.append(self)

    def hop(self):
        for _ in self.ring.hops(self.part):
            self.air.append(self.ring.send((self.state + self.air)[-1]))
        self.part += 1

    def land(self):
        self.state = self.state + self.air
        self.air = []

    def take(self):
        return jnp.concatenate(self.take_blocks(), axis=1)

    def take_blocks(self):
        self.ring.transfers.remove(self)
        return self.blocks()

    def blocks(self):
        ring = self.ring
        blocks = []
        for block in range(ring.count):
            chosen = self.state[0]
            at = ring.order.index(block)
            for device in range(ring.count):
                back = (ring.order.index(device) - at) % ring.count
                if back:
                    chosen = jnp.where(ring.me == device, self.state[back], chosen)
            blocks.append(chosen)
        return blocks


class Scatter:
    def __init__(self, ring, partial):
        self.ring = ring
        self.state = [partial]
        self.part = 0
        ring.transfers.append(self)

    def block(self, back):
        ring, partial = self.ring, self.state[0]
        width = partial.shape[1] // ring.count
        index = ring.lookup(ring.order, (ring.place + ring.count - back) % ring.count)
        return lax.dynamic_slice_in_dim(partial, index * width, width, axis=1)

    def hop(self):
        for step in self.ring.hops(self.part):
            send = self.block(step)
            if step > 1:
                send = (send.astype(f32) + self.state[1].astype(f32)).astype(bf16)
            self.state = [self.state[0], self.ring.send(send)]
        self.air = self.state.pop()
        self.part += 1

    def land(self):
        self.state = [self.state[0], self.air]

    def take(self):
        self.ring.transfers.remove(self)
        return self.block(0).astype(f32) + self.state[1].astype(f32)


class Cube:
    def __init__(self, total, cut, count, ring):
        self.count = count
        self.me = lax.axis_index(DP)
        bits = list(range(1, count.bit_length() - 1))
        self.halves = [total[:, :cut], total[:, cut:]]
        self.state = []
        self.todo = [bits, bits[::-1]]
        self.left = [list(bits), list(bits)]
        ring.transfers.append(self)

    def pick(self, x, todo, left, flip):
        blocks = 2 ** len(left)
        size = x.shape[0] // blocks
        at = 1 << left.index(todo[0])
        high = (((self.me >> todo[0]) & 1) ^ flip) == 1
        rows = [
            jnp.where(high, x[(i + at) * size : (i + at + 1) * size], x[i * size : (i + 1) * size])
            for i in range(blocks)
            if not i & at
        ]
        return jnp.concatenate(rows, axis=0)

    def hop(self):
        self.air = [
            lax.ppermute(
                self.pick(x, todo, left, 1), DP, [(d, d ^ (1 << todo[0])) for d in range(self.count)]
            )
            for x, todo, left in zip(self.halves, self.todo, self.left)
        ]

    def land(self):
        self.state = self.air

    def add(self):
        halves = []
        for i in range(2):
            x, todo, left, got = self.halves[i], self.todo[i], self.left[i], self.state[i]
            total = self.pick(x, todo, left, 0).astype(f32) + got.astype(f32)
            self.left[i] = [bit for bit in left if bit != todo[0]]
            self.todo[i] = todo[1:]
            halves.append(total.astype(bf16) if self.todo[i] else total)
        self.halves, self.state = halves, []


class Sums:
    def __init__(self, ring, own):
        self.state = [own]
        self.step = 1
        ring.transfers.append(self)

    def around(self, count):
        own = self.state[0]
        self.air = [
            lax.ppermute(own, HEAD, [(d, (d + step) % count) for d in range(count)])
            for step in range(1, count)
        ]

    def double(self, count, times):
        total = self.state[0]
        for _ in range(times):
            if self.step < count:
                total = total + lax.ppermute(total, DP, [(d, d ^ self.step) for d in range(count)])
                self.step *= 2
        self.state, self.air = [], [total]

    def land(self):
        self.state = [sum(self.state + self.air)]


def body(
    block_input, cotangent, seq_count, attn_gain, w_query, w_key, w_value, w_gate,
    w_alpha, w_beta, conv_weight, decay_base, decay_bias, norm_gain, w_out, mlp_gain,
    w_mlp_gate, w_mlp_up, w_down, *, heads_count, groups_count,
):
    micro_count, row_count, width = block_input.shape
    ring = Ring(heads_count)
    every, a, b = ring.bag(), ring.bag(), ring.bag()
    micros = (a, b)
    index = {a: 0, b: 1}
    features = heads_count * width
    heads = decay_base.shape[0]
    hidden_units = w_down.shape[0]
    inner = w_query.shape[1]
    per_micro = row_count // SEQ
    decay = jnp.stack([decay_base, decay_bias])
    gain_row = norm_gain[None]
    attn_own = attn_gain.astype(f32)
    mlp_own = mlp_gain.astype(f32)
    core = lax.axis_index(DP) & 1

    def own_of(values):
        return lax.dynamic_slice_in_dim(values, ring.me * width, width, axis=values.ndim - 1)

    def live_rows(m):
        return (jnp.arange(row_count) // SEQ < seq_count[index[m], 0])[:, None]

    def inputs_own(m):
        return jnp.where(live_rows(m), block_input[index[m]], jnp.zeros((), bf16)).astype(f32)

    def grad_output(m):
        return jnp.where(live_rows(m), cotangent[index[m]], jnp.zeros((), bf16))

    def normalise(m, raw):
        m.low = jnp.where(live_rows(m), raw, jnp.zeros((), bf16))
        inputs = m.low.astype(f32)
        m.scale_in = lax.rsqrt(jnp.mean(inputs * inputs, -1, keepdims=True) + epsilon)
        m.normed = (inputs * m.scale_in * every.gains[:1]).astype(bf16)

    def project(m):
        m.pre = matmul(m.normed, every.w_in)

    def mix(m):
        m.mixed, *m.saved = mixer_forward(m.pre, conv_weight, decay, gain_row)

    def attend(m, mixed):
        m.hidden = m.low.astype(f32) + matmul(mixed, every.w_out)

    def normalise_mid(m):
        hidden = m.hidden
        m.scale_mid = lax.rsqrt(jnp.mean(hidden * hidden, -1, keepdims=True) + epsilon)
        m.normed_mid = (hidden * m.scale_mid * every.gains[1:]).astype(bf16)

    def expand(m):
        m.acts = matmul(m.normed_mid, every.w_up2)

    def activate(m):
        gate_act, up_act = m.acts[:, :hidden_units], m.acts[:, hidden_units:]
        del m.acts
        sig = jax.nn.sigmoid(gate_act)
        silu = gate_act * sig
        m.product = (silu * up_act).astype(bf16)
        grad_product = m.grad_product.astype(f32)
        del m.grad_product
        grad_gate = (grad_product * up_act * sig * (1.0 + gate_act * (1.0 - sig))).astype(bf16)
        grad_up = (grad_product * silu).astype(bf16)
        m.grad_acts = jnp.concatenate([grad_gate, grad_up], axis=1)

    def back_mid(m):
        m.part_mid = matmul_back(m.grad_acts, every.w_up2, bf16)

    def contract(m):
        m.part_out = matmul(m.product, w_down, bf16)

    def back_hidden(m, grad_mid):
        grad_mid = grad_mid.astype(f32)
        scale, gain = m.scale_mid, every.gains[1:]
        dot_mid = jnp.sum(grad_mid * gain * m.hidden, -1, keepdims=True)
        back = scale**3 * dot_mid / features
        out = grad_output(m)
        m.grad_low = (out.astype(f32) + scale * gain * grad_mid - m.hidden * back).astype(bf16)
        m.grad_hidden_own = (
            own_of(out).astype(f32) + scale * mlp_own * m.grad_mid_own - own_of(m.hidden) * back
        )
        m.grad_mixed = matmul_back(m.grad_low, w_out)

    def mix_back(m, sequence):
        slot = index[m] * per_micro + sequence
        every.grad_pre, every.wide, every.decays, dots = mixer_backward(
            m.pre, conv_weight, decay, gain_row, *m.saved, m.grad_mixed,
            every.wide if slot else jnp.zeros((16, inner), f32),
            every.decays if slot else jnp.zeros((2, heads), f32),
            sequence, every.grad_pre if slot else None, slot, micro_count * per_micro,
        )
        m.dots = (m.dots if sequence else []) + [dots]

    def back_in(m):
        grad_pre = every.grad_pre[index[m] * row_count : (index[m] + 1) * row_count]
        m.part_in = matmul_back(grad_pre, every.w_in, bf16)

    def gain_in(m):
        m.gain_in = jnp.sum(m.part_in.astype(f32) * m.low.astype(f32) * m.scale_in, 0)

    def finish_output(m, summed):
        m.output = (own_of(m.hidden) + summed).astype(bf16)

    def finish_input(m, grad_in, dot_in):
        m.input_grad = (
            m.grad_hidden_own
            + m.scale_in * attn_own * grad_in
            - inputs_own(m) * m.scale_in**3 * dot_in[:, None] / features
        )

    def rows_of(former, latter):
        return jnp.concatenate([former, latter], axis=0)

    def by_core(rows, which):
        size = features // groups_count
        return jnp.concatenate(
            [
                jnp.where(which == 1, rows[:, at + size : at + 2 * size], rows[:, at : at + size])
                for at in range(0, features, 2 * size)
            ],
            axis=1,
        )

    in_a = ring.gather(block_input[0])
    slice_rows = w_out.shape[0] // groups_count
    gains = ring.gather(jnp.stack([attn_gain, mlp_gain]))
    shares = ring.gather(
        lax.dynamic_slice_in_dim(w_out, lax.axis_index(DP) * slice_rows, slice_rows, axis=0)
    )
    every.blocks = block_input
    gains.hop()
    in_a.hop()
    shares.hop()
    pad = jnp.zeros((features, CH - 2 * heads), bf16)
    last = lax.optimization_barrier(jnp.concatenate([w_alpha, w_beta, pad], axis=1))
    every.w_in = jnp.concatenate([w_query, w_key, w_value, w_gate, last], axis=1)
    ring.tick(in_a, shares, gains)
    in_b = ring.gather(every.blocks[1])
    del every.blocks
    gains.hop()
    in_a.hop()
    shares.hop()
    for m in micros:
        m.grad_product = matmul_back(grad_output(m), w_down, bf16)
    ring.tick(in_a, shares, gains)
    gains.hop()
    in_a.hop()
    ring.tick(in_a, gains)
    in_b.hop()
    shares.hop()
    every.gains = gains.take().astype(f32)
    normalise(a, in_a.take())
    project(a)
    ring.tick(in_b, shares)
    in_b.hop()
    w_out_full = lax.all_gather(
        jnp.stack(shares.take_blocks()), DP, axis=1, tiled=True
    ).reshape(-1, features)
    mix(a)
    every.w_ups = [w_mlp_gate, w_mlp_up]
    ring.tick(in_b)
    in_b.hop()
    mixed_a = ring.gather(a.mixed)
    mixed_a.hop()
    every.w_up2 = jnp.concatenate(every.w_ups, axis=1)
    del every.w_ups
    ring.tick(in_b)
    normalise(b, in_b.take())
    project(b)
    ring.tick(mixed_a)
    mixed_a.hop()
    mix(b)
    ring.tick(mixed_a)
    mixed_a.hop()
    mixed_b = ring.gather(b.mixed)
    mixed_b.hop()
    every.w_out = w_out_full
    ring.tick(mixed_a)
    attend(a, mixed_a.take())
    ring.tick(mixed_b)
    mixed_b.hop()
    normalise_mid(a)
    expand(a)
    ring.tick(mixed_b)
    mixed_b.hop()
    activate(a)
    back_mid(a)
    ring.tick(mixed_b)
    mid_a = ring.scatter(a.part_mid)
    del a.part_mid
    mid_a.hop()
    attend(b, mixed_b.take())
    ring.tick(mid_a)
    del every.w_out
    mid_a.hop()
    normalise_mid(b)
    expand(b)
    ring.tick(mid_a)
    mid_a.hop()
    activate(b)
    ring.tick(mid_a)
    a.grad_mid_own = mid_a.take()
    back_a = ring.gather(a.grad_mid_own.astype(bf16))
    back_a.hop()
    back_mid(b)
    ring.tick()
    mid_b = ring.scatter(b.part_mid)
    del b.part_mid
    mid_b.hop()
    every.down = matmul_rows(
        rows_of(a.product, b.product), rows_of(grad_output(a), grad_output(b)), bf16
    )
    ring.tick(back_a)
    down_sum = lax.psum_scatter(every.down, DP, scatter_dimension=1, tiled=True)
    del every.down
    back_a.hop()
    every.up2 = matmul_rows(
        rows_of(a.normed_mid, b.normed_mid), rows_of(a.grad_acts, b.grad_acts), bf16
    )
    ring.tick(mid_b)
    del a.normed_mid, b.normed_mid, a.grad_acts, b.grad_acts
    mid_b.hop()
    contract(a)
    contract(b)
    ring.tick(back_a)
    del a.product, b.product
    back_a.hop()
    normed = rows_of(a.normed, b.normed)
    every.normed_away = by_core(normed, 1 - core)
    every.normed_here = by_core(normed, core)
    ring.tick(mid_b)
    del a.normed, b.normed
    mid_b.hop()
    ring.tick(back_a)
    back_hidden(a, back_a.take())
    ring.tick(mid_b)
    b.grad_mid_own = mid_b.take()
    back_b = ring.gather(b.grad_mid_own.astype(bf16))
    back_b.hop()
    mix_back(a, 0)
    every.down_sum = down_sum
    ring.tick(back_b)
    up2_sum = lax.psum_scatter(every.up2, DP, scatter_dimension=0, tiled=True)
    del every.up2
    back_b.hop()
    for sequence in range(1, per_micro):
        mix_back(a, sequence)
    ring.tick(back_b)
    back_b.hop()
    back_in(a)
    ring.tick(back_b)
    out_a = ring.scatter(a.part_out)
    del a.part_out
    out_a.hop()
    back_hidden(b, back_b.take())
    ring.tick()
    in_grad_a = ring.scatter(a.part_in)
    in_grad_a.hop()
    mix_back(b, 0)
    ring.tick(out_a)
    out_a.hop()
    for sequence in range(1, per_micro):
        mix_back(b, sequence)
    ring.tick(in_grad_a)
    in_grad_a.hop()
    every.away = row_major(matmul_rows(every.normed_away, every.grad_pre, bf16))
    ring.tick(out_a)
    del every.normed_away
    out_a.hop()
    got = lax.ppermute(every.away, DP, [(d, d ^ 1) for d in range(groups_count)])
    del every.away
    back_in(b)
    every.up2_sum = up2_sum
    ring.tick(in_grad_a)
    in_grad_a.hop()
    every.total = row_major(
        (matmul_rows(every.normed_here, every.grad_pre) + got.astype(f32)).astype(bf16)
    )
    ring.tick(out_a)
    del every.normed_here, every.grad_pre
    cube = Cube(every.total, 2 * inner, groups_count, ring)
    del every.total
    cube.hop()
    out_b = ring.scatter(b.part_out)
    del b.part_out
    out_b.hop()
    every.out = matmul_rows(rows_of(a.mixed, b.mixed), rows_of(a.grad_low, b.grad_low), bf16)
    gain_in(a)
    gain_in(b)
    ring.tick(in_grad_a)
    del a.mixed, b.mixed, a.grad_low, b.grad_low
    out_sum = lax.psum_scatter(every.out, DP, scatter_dimension=1, tiled=True)
    del every.out
    in_grad_b = ring.scatter(b.part_in)
    in_grad_b.hop()
    del a.part_in, b.part_in
    taps = 3 * TAPS
    dots = jnp.concatenate(
        [jnp.concatenate(m.dots, axis=0) / m.scale_in for m in micros], axis=0
    ).reshape(-1)
    sums = Sums(
        ring,
        jnp.concatenate(
            [
                dots, a.gain_in + b.gain_in,
                jnp.sum(every.wide[taps].reshape(heads, CH), 0),
            ]
        ),
    )
    sums.around(heads_count)
    every.mlp_gain = jnp.sum(a.grad_mid_own * own_of(a.hidden) * a.scale_mid, 0) + jnp.sum(
        b.grad_mid_own * own_of(b.hidden) * b.scale_mid, 0
    )
    ring.tick(out_b)
    out_b.hop()
    every.down_grad = every.down_sum.astype(f32)
    every.up2_grad = [
        every.up2_sum[:, :hidden_units].astype(f32), every.up2_sum[:, hidden_units:].astype(f32)
    ]
    del every.down_sum, every.up2_sum
    finish_output(a, out_a.take())
    ring.tick(in_grad_b, sums, cube)
    in_grad_b.hop()
    cube.add()
    while cube.todo[0]:
        cube.hop()
        if len(cube.todo[0]) == 1:
            break
        cube.land()
        cube.add()
    [around] = sums.state
    small = Sums(
        ring,
        jnp.concatenate(
            [
                every.wide[:taps].reshape(-1),
                own_of(around[2 * row_count : 2 * row_count + features]),
                every.mlp_gain,
                jnp.pad(around[2 * row_count + features :], (0, inner - CH)),
                jnp.pad(every.decays.reshape(-1), (0, inner - 2 * heads)),
            ]
        ).reshape(-1, CH),
    )
    small.double(groups_count, 1)
    ring.tick(out_b, small)
    out_b.hop()
    finish_input(a, in_grad_a.take(), around[:row_count])
    ring.tick(in_grad_b, cube)
    in_grad_b.hop()
    small.double(groups_count, groups_count)
    cube.add()
    every.out_sum = out_sum
    ring.tick(out_b, small)
    out_grad = every.out_sum.astype(f32)
    finish_output(b, out_b.take())
    every.outputs = jnp.stack([m.output for m in micros])
    ring.tick(in_grad_b)
    finish_input(b, in_grad_b.take(), around[row_count : 2 * row_count])
    in_query_key, in_others = cube.halves
    small = small.state[0].reshape(-1)
    at = taps * inner
    return (
        every.outputs,
        jnp.stack([m.input_grad for m in micros]),
        small[at : at + width],
        in_query_key[:, :inner],
        in_query_key[:, inner:],
        in_others[:, :inner],
        in_others[:, inner : 2 * inner],
        in_others[:, 2 * inner : 2 * inner + heads],
        in_others[:, 2 * inner + heads : 2 * inner + 2 * heads],
        small[:at].reshape(3, TAPS, inner),
        small[at + 2 * width + inner : at + 2 * width + inner + heads],
        small[at + 2 * width + inner + heads : at + 2 * width + inner + 2 * heads],
        small[at + 2 * width : at + 2 * width + CH],
        out_grad,
        small[at + width : at + 2 * width],
        *every.up2_grad,
        every.down_grad,
    )


def solution(mesh):
    each = P(None, HEAD)
    return jax.shard_map(
        functools.partial(body, heads_count=mesh.shape[HEAD], groups_count=mesh.shape[DP]),
        mesh=mesh,
        in_specs=(
            P(None, DP, HEAD), P(None, DP, None), P(None, DP), P(HEAD),
            each, each, each, each, each, each, P(None, None, HEAD), P(HEAD), P(HEAD),
            P(), P(HEAD, None), P(HEAD), each, each, P(HEAD, None),
        ),
        out_specs=(
            P(None, DP, HEAD), P(None, DP, HEAD), P(HEAD),
            P(DP, HEAD), P(DP, HEAD), P(DP, HEAD), P(DP, HEAD),
            P(DP, HEAD), P(DP, HEAD), P(None, None, HEAD), P(HEAD), P(HEAD),
            P(), P(HEAD, DP), P(HEAD), P(DP, HEAD), P(DP, HEAD), P(HEAD, DP),
        ),
        check_vma=False,
    )
```
